512 devices in a mesh: tm: 8 (over y), acct: 64 (over z, x, core).
Axes of the slice: x: 4, y: 8, z: 8, core: 2. Of those that a mesh axis runs over, the one named last changes fastest.
Arguments:
- features: bfloat16 [8, 8192, 256], P('tm', 'acct'), may hold values from -6 to 6
- nbr_owner: int32 [8, 65536, 1], P('tm', 'acct'), may hold values from 0 to 63; in each aligned block of 1024 rows (0 to 1023, 1024 to 2047, ..., all dimensions but the last counted through in order) at most 20 rows name the same one
- nbr_row: int32 [8, 65536], P('tm', 'acct'), may hold values from 0 to 127
- counts: int32 [8, 8192], P('tm', 'acct'), may hold values from 1 to 8
- weight_one: bfloat16 [256, 256], replicated, may hold values from -0.375 to 0.375
- weight_two: bfloat16 [256, 256], replicated, may hold values from -0.375 to 0.375
- w_in: bfloat16 [256, 1024], replicated, may hold values from -0.375 to 0.375
- w_rec: bfloat16 [256, 1024], replicated, may hold values from -0.375 to 0.375
- gate_bias: float32 [1024], replicated, may hold values from -1 to 3
- cotangent: bfloat16 [8, 8192, 256], P('tm', 'acct'), may hold values from -6 to 6
Outputs:
- hidden: bfloat16 [8, 8192, 256], P('tm', 'acct')
- grad_gates: bfloat16 [8, 8192, 1024], P('tm', 'acct')
The draws below stay inside these ranges and needn't reach their ends.
Inputs may be any that keep to these rules, and one draw needn't show every extreme that they name: `nbr_owner`: in each aligned block of 1024 rows of one snapshot, no shard is named more than 20 times, a bound that some block reaches.
All inputs are finite; a program needn't handle non-finite values.
Results may differ from the reference program's by a relative error of at most 0.014.
Values may be sent and summed in bfloat16 or wider, within the bound.
No kernel may reach another device: no remote copies, remote signals or barrier semaphores. Data moves between devices by JAX's collectives and lax.ppermute only.
A program may use at most 64 MiB of HBM per device.

```python
import math
import jax
import jax.numpy as jnp
import numpy as np

H = 256
KNB = 8
NODE_DEV = 128
SNAPS = 8
NODES = 8192
CAP = 20
N_ACCT = 64


def set_ends(result, own_key, least, high):
    longest = result.shape.index(max(result.shape))
    spots = []
    for shift in (0, 1):
        where = [jax.random.randint(jax.random.fold_in(own_key, axis), (), 0, length) for axis, length in enumerate(result.shape)]
        where[longest] = (where[longest] + shift) % result.shape[longest]
        spots.append(tuple(where))
    return result.at[spots[0]].set(least).at[spots[1]].set(high)


def block_levels(key, shape, shards, least, largest):
    def one(position, blocks):
        steps = jax.random.uniform(jax.random.fold_in(jax.random.fold_in(key, 6), position), (blocks,), jnp.float32, least / len(shards), largest / len(shards))
        return jnp.repeat(jnp.exp(steps), shape[position] // blocks).reshape((-1,) + (1,) * (len(shape) - position - 1))

    factor_of = one(*shards[0])
    for cut in shards[1:]:
        factor_of = factor_of * one(*cut)
    return factor_of


def deal_out(key, own, number, rows, number_of, top, reach, lean):
    sequence = jax.random.permutation(key, number_of)
    packed, usual = portions_of(number_of, rows * top, reach, lean, True), portions_of(number_of, rows * top, reach, lean, False)
    places = jnp.arange(number_of)

    def named(lengths, turn):
        used = int((lengths > 0).sum())
        fixed = max(1, used // 4)
        moved = fixed + (places - fixed + turn * (used - fixed)) % max(1, number_of - fixed)
        return jnp.zeros((number_of,), jnp.int32).at[sequence[jnp.where(places < fixed, places, moved)]].set(jnp.asarray(lengths, jnp.int32))

    lengths = jnp.where(number % 4 == 0, named(packed, number // 4), named(usual, number - number // 4 - 1))
    mixed = jax.random.permutation(jax.random.fold_in(own, 3), number_of)
    donor, taker = mixed[0:number_of // 2 * 2:2], mixed[1:number_of // 2 * 2:2]
    slack = jnp.minimum(lengths[donor] - 1, reach - lengths[taker]) // 2
    slack = jnp.where((donor == sequence[0]) | (taker == sequence[0]) | (lengths[taker] == 0), 0, jnp.maximum(slack, 0))
    moved = jax.random.randint(jax.random.fold_in(own, 4), (number_of // 2,), 0, 1 << 20) % (slack + 1)
    lengths = lengths.at[donor].add(-moved).at[taker].add(moved)
    items = jnp.searchsorted(jnp.cumsum(lengths), jnp.arange(rows * top), side="right").astype(jnp.int32)
    grid = items.reshape(top, rows).T
    grid = grid[jax.random.permutation(jax.random.fold_in(own, 1), rows)]
    turn = jax.random.randint(jax.random.fold_in(own, 2), (rows, 1), 0, top)
    return jnp.take_along_axis(grid, (jnp.arange(top)[None, :] + turn) % top, axis=1)


def portions_of(count, total, bound, lean, full):
    portions = [(1 << 20) // math.isqrt(grade ** lean) + 1 for grade in range(1, count + 1)]
    largest = bound if full else min(bound, max(-(-total // count), total * portions[0] // sum(portions)))
    least = 1 if total - largest >= count - 1 else 0
    given, surplus = [largest] + [least] * (count - 1), total - largest - least * (count - 1)
    while surplus > 0:
        free = [i for i in range(1, count) if given[i] < largest] or [i for i in range(1, count) if given[i] < bound]
        pool, remaining = sum([portions[i] for i in free]), surplus
        for i in free:
            more = min(bound - given[i], max(1, remaining * portions[i] // pool), surplus)
            given[i] = given[i] + more
            surplus = surplus - more
    return np.array(given)


def gaussian(key, dims, deviation, limit, cuts=(), kind=jnp.bfloat16):
    drawn = jax.random.normal(key, dims, jnp.float32) * deviation
    if len(cuts) > 0:
        drawn = block_levels(key, dims, cuts, -0.22, 0.18) * drawn
    return jnp.clip(drawn, min=-limit, max=limit).astype(kind)


def setup_inputs(seed: int = 0) -> dict:
    arg_keys = jax.random.split(jax.random.key(seed), 11)
    features = gaussian(arg_keys[0], (SNAPS, NODES, H), 1.0, 6.0, ((0, 8), (1, 64)))
    nbr_owner_keys = jax.random.split(jax.random.fold_in(arg_keys[1], 1), SNAPS * (NODES * KNB) // (NODE_DEV * KNB))
    nbr_owner_turns = jax.random.permutation(jax.random.fold_in(arg_keys[1], 3), SNAPS * (NODES * KNB) // (NODE_DEV * KNB))
    nbr_owner = jax.vmap(lambda own, number: deal_out(jax.random.fold_in(arg_keys[1], 2), own, number, NODE_DEV * KNB, N_ACCT, 1, CAP, 2))(nbr_owner_keys, nbr_owner_turns).reshape((SNAPS, NODES * KNB, 1))
    nbr_row = set_ends(jax.random.randint(arg_keys[2], (SNAPS, NODES * KNB), 0, NODE_DEV), jax.random.fold_in(arg_keys[2], 1), 0, NODE_DEV - 1).astype(jnp.int32)
    counts = set_ends(jax.random.randint(arg_keys[3], (SNAPS, NODES), 1, KNB + 1), jax.random.fold_in(arg_keys[3], 1), 1, KNB).astype(jnp.int32)
    weight_one = gaussian(arg_keys[4], (H, H), H ** -0.5, 0.375)
    weight_two = gaussian(arg_keys[5], (H, H), H ** -0.5, 0.375)
    w_in = gaussian(arg_keys[6], (H, 4 * H), H ** -0.5, 0.375)
    w_rec = gaussian(arg_keys[7], (H, 4 * H), H ** -0.5, 0.375)
    gate_bias = jnp.clip(jax.random.uniform(arg_keys[8], (4 * H,), jnp.float32, -1.0, 3.0), -1.0, 3.0)
    cotangent = gaussian(arg_keys[9], (SNAPS, NODES, H), 1.0, 6.0, ((0, 8), (1, 64)))
    return dict(features=features, nbr_owner=nbr_owner, nbr_row=nbr_row, counts=counts, weight_one=weight_one, weight_two=weight_two, w_in=w_in, w_rec=w_rec, gate_bias=gate_bias, cotangent=cotangent)


def cell(z, h_prev, c_prev, w_rec):
    gates = z.astype(jnp.float32) + jnp.dot(h_prev, w_rec, preferred_element_type=jnp.float32)
    gate_i = jax.nn.sigmoid(gates[:, :H])
    gate_f = jax.nn.sigmoid(gates[:, H:2 * H])
    gate_g = jnp.tanh(gates[:, 2 * H:3 * H])
    gate_o = jax.nn.sigmoid(gates[:, 3 * H:])
    cell_new = gate_f * c_prev + gate_i * gate_g
    return (gate_o * jnp.tanh(cell_new)).astype(jnp.bfloat16), cell_new


def backstep(z, h_prev, c_prev, grad_h, grad_c, w_rec):
    gates = z.astype(jnp.float32) + jnp.dot(h_prev, w_rec, preferred_element_type=jnp.float32)
    gate_i = jax.nn.sigmoid(gates[:, :H])
    gate_f = jax.nn.sigmoid(gates[:, H:2 * H])
    gate_g = jnp.tanh(gates[:, 2 * H:3 * H])
    gate_o = jax.nn.sigmoid(gates[:, 3 * H:])
    cell_new = gate_f * c_prev + gate_i * gate_g
    tanh_c = jnp.tanh(cell_new)
    grad_o = grad_h * tanh_c
    total_c = grad_c + grad_h * gate_o * (1.0 - tanh_c * tanh_c)
    pieces = [total_c * gate_g * gate_i * (1.0 - gate_i),
              total_c * c_prev * gate_f * (1.0 - gate_f),
              total_c * gate_i * (1.0 - gate_g * gate_g),
              grad_o * gate_o * (1.0 - gate_o)]
    grad_g = jnp.concatenate(pieces, 1).astype(jnp.bfloat16)
    grad_hp = jnp.einsum("ng,hg->nh", grad_g, w_rec, preferred_element_type=jnp.float32)
    return grad_g, grad_hp, total_c * gate_f


def convolve(x, global_ids, mask, scale, weight):
    picked = x[global_ids].reshape(NODES, KNB, H).astype(jnp.float32)
    summed = x.astype(jnp.float32) + jnp.sum(picked * mask[:, :, None], 1)
    agg = (summed * scale[:, None]).astype(jnp.bfloat16)
    return jax.nn.relu(jnp.dot(agg, weight, preferred_element_type=jnp.float32)).astype(jnp.bfloat16)


def reference(features, nbr_owner, nbr_row, counts, weight_one, weight_two, w_in, w_rec, gate_bias, cotangent):
    h_now = jnp.zeros((NODES, H), jnp.bfloat16)
    c_now = jnp.zeros((NODES, H), jnp.float32)
    saved = []
    hidden_list = []
    for snap in range(SNAPS):
        global_ids = (nbr_owner[snap, :, 0] * NODE_DEV + nbr_row[snap]).astype(jnp.int32)
        cnt = counts[snap]
        mask = (jnp.arange(KNB, dtype=jnp.int32)[None, :] < cnt[:, None]).astype(jnp.float32)
        scale = 1.0 / (cnt.astype(jnp.float32) + 1.0)
        first = convolve(features[snap], global_ids, mask, scale, weight_one)
        second = convolve(first, global_ids, mask, scale, weight_two)
        z = (jnp.dot(second, w_in, preferred_element_type=jnp.float32) + gate_bias).astype(jnp.bfloat16)
        saved.append((z, h_now, c_now))
        h_now, c_now = cell(z, h_now, c_now, w_rec)
        hidden_list.append(h_now)
    grad_h = jnp.zeros((NODES, H), jnp.float32)
    grad_c = jnp.zeros((NODES, H), jnp.float32)
    grad_list = [None] * SNAPS
    for snap in range(SNAPS - 1, -1, -1):
        z, h_prev, c_prev = saved[snap]
        grad_g, grad_h, grad_c = backstep(z, h_prev, c_prev, cotangent[snap].astype(jnp.float32) + grad_h, grad_c, w_rec)
        grad_list[snap] = grad_g
    return jnp.stack(hidden_list), jnp.stack(grad_list)
```

```python
import jax
import jax.numpy as jnp
from jax import lax
from jax.experimental import pallas as pl
from jax.experimental.pallas import tpu as pltpu
from jax.sharding import Mesh
from jax.sharding import PartitionSpec as P

H = 256
KNB = 8
NODE = 128
SNAPS = 8
CHIPS = 32
CAP = 40
LANES = 128
PART = NODE // SNAPS
SLOTS = CHIPS * CAP
VMEM = pltpu.CompilerParams(vmem_limit_bytes=32 * 1024 * 1024)
BF16 = jnp.bfloat16
F32 = jnp.float32


def iota(shape, dim):
    return lax.broadcasted_iota(jnp.int32, shape, dim)


def matmul(a, b, dims=((1,), (0,))):
    return lax.dot_general(a, b, (dims, ((), ())), preferred_element_type=F32)


NT = ((1,), (1,))


def plan_kernel(owner_ref, row_ref, cnt_ref, wanted_ref, comb_ref):
    owner = owner_ref[...]
    value = ((owner % 2) * NODE + row_ref[...]).astype(F32)
    chip = owner // 2
    upper = jnp.where(iota((LANES, LANES), 0) < iota((LANES, LANES), 1), 1.0, 0.0).astype(BF16)
    base = jnp.zeros((CHIPS, 1), F32)
    wanted = jnp.zeros((CHIPS, LANES), F32)
    where = jnp.zeros((NODE, 2 * KNB), F32)
    lane = iota((1, LANES), 1)
    for i in range(KNB):
        chip_i = chip[i : i + 1, :]
        onehot = jnp.where(iota((CHIPS, LANES), 0) == chip_i, 1.0, 0.0)
        before = matmul(onehot.astype(BF16), upper) + base
        base = base + jnp.sum(onehot, 1, keepdims=True)
        rank = jnp.sum(onehot * before, 0, keepdims=True)
        ranks = jnp.where(iota((LANES, LANES), 0).astype(F32) == rank, 1.0, 0.0).astype(BF16)
        wanted = wanted + matmul((onehot * value[i : i + 1, :]).astype(BF16), ranks, NT)
        group = jnp.where(iota((NODE, LANES), 0) == i * (LANES // KNB) + lane // KNB, 1.0, 0.0)
        sub = iota((2 * KNB, LANES), 0)
        coded = jnp.where(
            sub % KNB == lane % KNB, jnp.where(sub < KNB, chip_i.astype(F32), rank), 0.0
        )
        where = where + matmul(group.astype(BF16), coded.astype(BF16), NT)
    wanted_ref[...] = wanted
    eye = iota((NODE, NODE), 0) == iota((NODE, NODE), 1)
    count = jnp.sum(jnp.where(eye, cnt_ref[...].astype(F32), 0.0), 1, keepdims=True)
    place = where[:, :KNB] * CAP + where[:, KNB:]
    place = jnp.where(iota((NODE, KNB), 1).astype(F32) < count, place, -1.0)
    spot = iota((NODE, SLOTS), 1).astype(F32)
    comb = jnp.zeros((NODE, SLOTS), F32)
    for k in range(KNB):
        comb = comb + jnp.where(spot == place[:, k : k + 1], 1.0, 0.0)
    comb_ref[...] = comb.astype(BF16)


def pick_kernel(asked_ref, x_ref, pick_ref, out_ref):
    eye = jnp.where(iota((LANES, LANES), 0) == iota((LANES, LANES), 1), 1.0, 0.0).astype(BF16)
    turned = matmul(eye, asked_ref[...].astype(BF16), NT)
    col = iota((CAP, H), 1).astype(F32)
    x = x_ref[...]
    for d in range(0, CHIPS, 2):
        both = [jnp.where(turned[:CAP, e : e + 1] == col, 1.0, 0.0) for e in (d, d + 1)]
        pick = jnp.concatenate(both, 0).astype(BF16)
        pick_ref[d * CAP : (d + 2) * CAP, :] = pick
        out_ref[d * CAP : (d + 2) * CAP, :] = matmul(pick, x).astype(BF16)


def again_kernel(pick_ref, x_ref, out_ref):
    out_ref[...] = matmul(pick_ref[...], x_ref[...]).astype(BF16)


def conv_kernel(comb_ref, arrived_ref, x_ref, cnt_ref, weight_ref, out_ref):
    eye = iota((NODE, NODE), 0) == iota((NODE, NODE), 1)
    count = jnp.sum(jnp.where(eye, cnt_ref[...].astype(F32), 0.0), 1, keepdims=True)
    summed = x_ref[...].astype(F32) + matmul(comb_ref[...], arrived_ref[...])
    agg = (summed * (1.0 / (count + 1.0))).astype(BF16)
    out_ref[...] = jnp.maximum(matmul(agg, weight_ref[...]), 0.0).astype(BF16)


def lstm_kernel(xc_ref, w_in_ref, w_rec_ref, bias_ref, out_ref, z_ref, saved_ref):
    x = xc_ref[:, :, :H].reshape(NODE, H)
    z = matmul(x, w_in_ref[...]) + bias_ref[...]
    z_ref[...] = z.astype(BF16).astype(F32)
    h = None
    c = jnp.zeros((PART, H), F32)
    for t in range(SNAPS):
        gates = z_ref[t * PART : (t + 1) * PART, :]
        if t > 0:
            gates = gates + matmul(h, w_rec_ref[...])
        i = jax.nn.sigmoid(gates[:, :H])
        f = jax.nn.sigmoid(gates[:, H : 2 * H])
        g = jnp.tanh(gates[:, 2 * H : 3 * H])
        o = jax.nn.sigmoid(gates[:, 3 * H :])
        c_new = f * c + i * g
        tc = jnp.tanh(c_new)
        h = (o * tc).astype(BF16)
        out_ref[t, :, :H] = h
        saved_ref[t, 0] = f
        saved_ref[t, 1] = o * (1.0 - tc * tc)
        saved_ref[t, 2] = g * i * (1.0 - i)
        saved_ref[t, 3] = c * f * (1.0 - f)
        saved_ref[t, 4] = i * (1.0 - g * g)
        saved_ref[t, 5] = tc * o * (1.0 - o)
        c = c_new
    dh = jnp.zeros((PART, H), F32)
    dc = jnp.zeros((PART, H), F32)
    for t in range(SNAPS - 1, -1, -1):
        dh = dh + xc_ref[t, :, H:].astype(F32)
        dc = dc + dh * saved_ref[t, 1]
        grad = jnp.concatenate(
            [dc * saved_ref[t, 2], dc * saved_ref[t, 3], dc * saved_ref[t, 4], dh * saved_ref[t, 5]],
            1,
        ).astype(BF16)
        out_ref[t, :, H:] = grad
        if t > 0:
            dh = matmul(grad, w_rec_ref[...], NT)
            dc = dc * saved_ref[t, 0]


def call(kernel, out, *args, scratch=()):
    return pl.pallas_call(
        kernel, out_shape=out, scratch_shapes=list(scratch), compiler_params=VMEM
    )(*args)


def shaped(shape, dtype=BF16):
    return jax.ShapeDtypeStruct(shape, dtype)


def shards(
    features, nbr_owner, nbr_row, counts, weight_one, weight_two, w_in, w_rec, gate_bias, cotangent
):
    x = features[0]
    chips = ("z", "x")
    wanted, comb = call(
        plan_kernel,
        (shaped((CHIPS, LANES), F32), shaped((NODE, SLOTS))),
        nbr_owner.reshape(KNB, LANES),
        nbr_row.reshape(KNB, LANES),
        counts,
    )
    asked = lax.all_to_all(wanted, chips, 0, 0, tiled=True)
    pair = lax.all_gather(x, "core", tiled=True)
    pick, outgoing = call(
        pick_kernel, (shaped((SLOTS, H)), shaped((SLOTS, H))), asked, pair
    )
    arrived = lax.all_to_all(outgoing, chips, 0, 0, tiled=True)
    x = call(conv_kernel, shaped((NODE, H)), comb, arrived, x, counts, weight_one)
    pair = lax.all_gather(x, "core", tiled=True)
    outgoing = call(again_kernel, shaped((SLOTS, H)), pick, pair)
    arrived = lax.all_to_all(outgoing, chips, 0, 0, tiled=True)
    x = call(conv_kernel, shaped((NODE, H)), comb, arrived, x, counts, weight_two)
    both = jnp.concatenate([x, cotangent[0]], 1).reshape(SNAPS, PART, 2 * H)
    both = lax.all_to_all(both, "tm", 0, 0, tiled=True)
    result = call(
        lstm_kernel,
        shaped((SNAPS, PART, 5 * H)),
        both,
        w_in,
        w_rec,
        gate_bias.reshape(1, 4 * H),
        scratch=(pltpu.VMEM((NODE, 4 * H), F32), pltpu.VMEM((SNAPS, 6, PART, H), F32)),
    )
    result = lax.all_to_all(result, "tm", 0, 0, tiled=True).reshape(1, NODE, 5 * H)
    return result[:, :, :H], result[:, :, H:]


def solution(mesh):
    mesh = Mesh(mesh.devices.reshape(8, 8, 4, 2), ("tm", "z", "x", "core"))
    acct = ("z", "x", "core")
    return jax.shard_map(
        shards,
        mesh=mesh,
        in_specs=(
            P("tm", acct, None),
            P("tm", acct, None),
            P("tm", acct),
            P("tm", acct),
            P(),
            P(),
            P(),
            P(),
            P(),
            P("tm", acct, None),
        ),
        out_specs=(P("tm", acct, None), P("tm", acct, None)),
        check_vma=False,
    )
```

```python
import jax
import jax.numpy as jnp
from jax import lax
from jax.experimental import pallas as pl
from jax.experimental.pallas import tpu as pltpu
from jax.sharding import Mesh
from jax.sharding import PartitionSpec as P

H = 256
KNB = 8
NODE = 128
SNAPS = 8
GROUP = 8
ROWS = GROUP * NODE
LANES = 128
PART = NODE // SNAPS
UNUSED = -1000000.0
VMEM = pltpu.CompilerParams(vmem_limit_bytes=40 * 1024 * 1024)
BF16 = jnp.bfloat16
F32 = jnp.float32
NT = ((1,), (1,))


def iota(shape, dim):
    return lax.broadcasted_iota(jnp.int32, shape, dim)


def matmul(a, b, dims=((1,), (0,))):
    return lax.dot_general(a, b, (dims, ((), ())), preferred_element_type=F32)


def list_kernel(owner_ref, row_ref, cnt_ref, out_ref):
    owner = owner_ref[...].astype(F32)
    row = row_ref[...].astype(F32)
    lane = iota((1, LANES), 1)
    sub = iota((2 * KNB, LANES), 0)
    listed = jnp.zeros((2 * KNB, NODE), F32)
    for i in range(KNB):
        group = jnp.where(iota((NODE, LANES), 0) == i * (LANES // KNB) + lane // KNB, 1.0, 0.0)
        coded = jnp.where(
            sub % KNB == lane % KNB,
            jnp.where(sub < KNB, owner[i : i + 1, :], row[i : i + 1, :]),
            0.0,
        )
        listed = listed + matmul(coded.astype(BF16), group.astype(BF16), NT)
    code = listed[:KNB] * NODE + listed[KNB:]
    code = jnp.where(iota((KNB, NODE), 0) < cnt_ref[...], code, UNUSED)
    for z in range(GROUP):
        out_ref[z] = code - z * ROWS


def adjacency_kernel(code_ref, place_ref, adj_ref, scale_ref):
    code = code_ref[...].reshape(GROUP * KNB, NODE)
    code = jnp.concatenate([code, jnp.full((NODE - GROUP * KNB, NODE), UNUSED, F32)], 0).T
    spot = iota((NODE, ROWS), 1).astype(F32)
    used = jnp.where(code > UNUSED / 2, 1.0, 0.0)
    for z in range(GROUP):
        adj = jnp.zeros((NODE, ROWS), F32)
        for k in range(KNB):
            at = z * KNB + k
            adj = adj + jnp.where(spot == code[:, at : at + 1], 1.0, 0.0)
        adj_ref[z * NODE : (z + 1) * NODE, :] = adj.astype(BF16)
        count = jnp.sum(used[:, z * KNB : (z + 1) * KNB], 1, keepdims=True)
        scale_ref[z * NODE : (z + 1) * NODE, :] = jnp.broadcast_to(
            1.0 / (count + 1.0), (NODE, LANES)
        )
    mine = pl.ds(pl.multiple_of(place_ref[0] * NODE, NODE), NODE)
    here = pl.ds(pl.multiple_of(place_ref[1] * NODE, NODE), NODE)
    eye = jnp.where(iota((NODE, NODE), 0) == iota((NODE, NODE), 1), 1.0, 0.0)
    adj_ref[mine, here] = (adj_ref[mine, here].astype(F32) + eye).astype(BF16)


def partial_kernel(adj_ref, plane_ref, scale_ref, out_ref):
    plane = plane_ref[...]
    for z in range(GROUP):
        rows = slice(z * NODE, (z + 1) * NODE)
        out_ref[rows, :] = (
            matmul(adj_ref[rows, :], plane) * scale_ref[rows, :1]
        ).astype(BF16)


def first_kernel(part_ref, weight_ref, out_ref):
    total = part_ref[0].astype(F32)
    for z in range(1, GROUP):
        total = total + part_ref[z].astype(F32)
    x = jnp.maximum(matmul(total.astype(BF16), weight_ref[...]), 0.0).astype(BF16)
    for z in range(GROUP):
        out_ref[z] = x


def lstm_kernel(
    part_ref, cot_ref, weight_ref, w_in_ref, w_rec_ref, bias_ref, out_ref, z_ref, saved_ref
):
    total = part_ref[0].astype(F32)
    for z in range(1, GROUP):
        total = total + part_ref[z].astype(F32)
    x = jnp.maximum(matmul(total.astype(BF16), weight_ref[...]), 0.0).astype(BF16)
    z_ref[...] = (matmul(x, w_in_ref[...]) + bias_ref[...]).astype(BF16).astype(F32)
    h = None
    c = jnp.zeros((PART, H), F32)
    for t in range(SNAPS):
        gates = z_ref[t * PART : (t + 1) * PART, :]
        if t > 0:
            gates = gates + matmul(h, w_rec_ref[...])
        i = jax.nn.sigmoid(gates[:, :H])
        f = jax.nn.sigmoid(gates[:, H : 2 * H])
        g = jnp.tanh(gates[:, 2 * H : 3 * H])
        o = jax.nn.sigmoid(gates[:, 3 * H :])
        c_new = f * c + i * g
        tc = jnp.tanh(c_new)
        h = (o * tc).astype(BF16)
        out_ref[t, :, :H] = h
        saved_ref[t, 0] = f
        saved_ref[t, 1] = o * (1.0 - tc * tc)
        saved_ref[t, 2] = g * i * (1.0 - i)
        saved_ref[t, 3] = c * f * (1.0 - f)
        saved_ref[t, 4] = i * (1.0 - g * g)
        saved_ref[t, 5] = tc * o * (1.0 - o)
        c = c_new
    dh = jnp.zeros((PART, H), F32)
    dc = jnp.zeros((PART, H), F32)
    for t in range(SNAPS - 1, -1, -1):
        dh = dh + cot_ref[t].astype(F32)
        dc = dc + dh * saved_ref[t, 1]
        grad = jnp.concatenate(
            [dc * saved_ref[t, 2], dc * saved_ref[t, 3], dc * saved_ref[t, 4], dh * saved_ref[t, 5]],
            1,
        ).astype(BF16)
        out_ref[t, :, H:] = grad
        if t > 0:
            dh = matmul(grad, w_rec_ref[...], NT)
            dc = dc * saved_ref[t, 0]


def call(kernel, out, *args, scratch=(), in_specs=None):
    more = {} if in_specs is None else {"in_specs": in_specs}
    return pl.pallas_call(
        kernel, out_shape=out, scratch_shapes=list(scratch), compiler_params=VMEM, **more
    )(*args)


def shaped(shape, dtype=BF16):
    return jax.ShapeDtypeStruct(shape, dtype)


def exchange(array, axes):
    return lax.all_to_all(array, axes, 0, 0, tiled=True)


def shards(
    features, nbr_owner, nbr_row, counts, weight_one, weight_two, w_in, w_rec, gate_bias, cotangent
):
    plane_axes = ("x", "core")
    place = jnp.stack([lax.axis_index("z"), lax.axis_index(plane_axes)]).astype(jnp.int32)
    copies = jnp.broadcast_to(features, (GROUP, NODE, H))
    plane = exchange(copies, plane_axes).reshape(ROWS, H)
    listed = call(
        list_kernel,
        shaped((GROUP, KNB, NODE), F32),
        nbr_owner.reshape(KNB, LANES),
        nbr_row.reshape(KNB, LANES),
        counts,
    )
    code = exchange(listed, "z")
    vmem = pl.BlockSpec(memory_space=pltpu.VMEM)
    adj, scale = call(
        adjacency_kernel,
        (shaped((ROWS, ROWS)), shaped((ROWS, LANES), F32)),
        code,
        place,
        in_specs=[vmem, pl.BlockSpec(memory_space=pltpu.SMEM)],
    )
    part = call(partial_kernel, shaped((ROWS, H)), adj, plane, scale)
    part = exchange(part.reshape(GROUP, NODE, H), "z")
    copies = call(first_kernel, shaped((GROUP, NODE, H)), part, weight_one)
    plane = exchange(copies, plane_axes).reshape(ROWS, H)
    part = call(partial_kernel, shaped((ROWS, H)), adj, plane, scale)
    part = exchange(part.reshape(GROUP * SNAPS, PART, H), ("z", "tm")).reshape(GROUP, NODE, H)
    cot = exchange(cotangent.reshape(SNAPS, PART, H), "tm")
    result = call(
        lstm_kernel,
        shaped((SNAPS, PART, 5 * H)),
        part,
        cot,
        weight_two,
        w_in,
        w_rec,
        gate_bias.reshape(1, 4 * H),
        scratch=(pltpu.VMEM((NODE, 4 * H), F32), pltpu.VMEM((SNAPS, 6, PART, H), F32)),
    )
    result = exchange(result, "tm").reshape(1, NODE, 5 * H)
    return result[:, :, :H], result[:, :, H:]


def solution(mesh):
    mesh = Mesh(mesh.devices.reshape(8, 8, 4, 2), ("tm", "z", "x", "core"))
    acct = ("z", "x", "core")
    return jax.shard_map(
        shards,
        mesh=mesh,
        in_specs=(
            P("tm", acct, None),
            P("tm", acct, None),
            P("tm", acct),
            P("tm", acct),
            P(),
            P(),
            P(),
            P(),
            P(),
            P("tm", acct, None),
        ),
        out_specs=(P("tm", acct, None), P("tm", acct, None)),
        check_vma=False,
    )
```

```python
import jax
import jax.numpy as jnp
from jax import lax
from jax.experimental import pallas as pl
from jax.experimental.pallas import tpu as pltpu
from jax.sharding import Mesh
from jax.sharding import PartitionSpec as P

H = 256
KNB = 8
NODE = 128
SNAPS = 8
GROUP = 8
ROWS = GROUP * NODE
LANES = 128
PART = NODE // SNAPS
CHIPS = 32
CAP = 40
SLOTS = CHIPS * CAP
BITS = 11
NONE = 2047
ASKED, COUNT = 4, 5
VMEM = pltpu.CompilerParams(vmem_limit_bytes=16 * 1024 * 1024)
BF16 = jnp.bfloat16
F32 = jnp.float32
NT = ((1,), (1,))


def iota(shape, dim):
    return lax.broadcasted_iota(jnp.int32, shape, dim)


def matmul(a, b, dims=((1,), (0,))):
    return lax.dot_general(a, b, (dims, ((), ())), preferred_element_type=F32)


def plan_kernel(owner_hbm, row_hbm, cnt_hbm, msg_ref, place_ref, owner_ref, row_ref, cnt_ref, sems):
    pairs = ((owner_hbm, owner_ref), (row_hbm, row_ref), (cnt_hbm, cnt_ref))
    copies = [
        pltpu.make_async_copy(a, b, sems.at[i]) for i, (a, b) in enumerate(pairs)
    ]
    for copy in copies:
        copy.start()
    for copy in copies:
        copy.wait()
    owner = owner_ref[...]
    value = ((owner % 2) * NODE + row_ref[...]).astype(F32)
    chip = owner // 2
    upper = jnp.where(iota((LANES, LANES), 0) < iota((LANES, LANES), 1), 1.0, 0.0).astype(BF16)
    base = jnp.zeros((CHIPS, 1), F32)
    wanted = jnp.zeros((CHIPS, LANES), F32)
    place = jnp.zeros((NODE, 2 * KNB), F32)
    listed = jnp.zeros((2 * KNB, NODE), F32)
    lane = iota((1, LANES), 1)
    sub = iota((2 * KNB, LANES), 0)
    for i in range(KNB):
        chip_i = chip[i : i + 1, :]
        value_i = value[i : i + 1, :]
        onehot = jnp.where(iota((CHIPS, LANES), 0) == chip_i, 1.0, 0.0)
        before = matmul(onehot.astype(BF16), upper) + base
        base = base + jnp.sum(onehot, 1, keepdims=True)
        rank = jnp.sum(onehot * before, 0, keepdims=True)
        ranks = jnp.where(iota((LANES, LANES), 0).astype(F32) == rank, 1.0, 0.0).astype(BF16)
        wanted = wanted + matmul((onehot * value_i).astype(BF16), ranks, NT)
        group = jnp.where(iota((NODE, LANES), 0) == i * (LANES // KNB) + lane // KNB, 1.0, 0.0)
        group = group.astype(BF16)
        mine = sub % KNB == lane % KNB
        coded = jnp.where(mine, jnp.where(sub < KNB, chip_i.astype(F32), rank), 0.0)
        place = place + matmul(group, coded.astype(BF16), NT)
        coded = jnp.where(mine, jnp.where(sub < KNB, chip_i.astype(F32), value_i), 0.0)
        listed = listed + matmul(coded.astype(BF16), group, NT)
    place_ref[...] = place
    wanted = wanted.astype(jnp.int32)
    count = cnt_ref[...]
    chip = listed[:KNB].astype(jnp.int32)
    code = (chip % 4) * (2 * NODE) + listed[KNB:].astype(jnp.int32)
    plane = jnp.where(iota((KNB, NODE), 0) < count, chip // 4, -1)
    blank = jnp.zeros((KNB - COUNT - 1, LANES), jnp.int32)
    for z in range(GROUP):
        here = jnp.where(plane == z, code, NONE)
        packed = here[: KNB // 2] * (1 << BITS) + here[KNB // 2 :]
        for x in range(4):
            at = z * 4 + x
            msg_ref[at] = jnp.concatenate([packed, wanted[at : at + 1], count, blank], 0)


def column(row):
    eye = iota((NODE, NODE), 0) == iota((NODE, NODE), 1)
    return jnp.sum(jnp.where(eye, row, 0.0), 1, keepdims=True)


def comb_kernel(place_ref, cnt_ref, comb_ref):
    count = column(cnt_ref[...].astype(F32))
    place = place_ref[:, :KNB] * CAP + place_ref[:, KNB:]
    place = jnp.where(iota((NODE, KNB), 1).astype(F32) < count, place, -1.0)
    spot = iota((NODE, SLOTS), 1).astype(F32)
    comb = jnp.zeros((NODE, SLOTS), F32)
    for k in range(KNB):
        comb = comb + jnp.where(spot == place[:, k : k + 1], 1.0, 0.0)
    comb_ref[...] = comb.astype(BF16)


def pick_kernel(msg_ref, x_ref, out_ref):
    eye = jnp.where(iota((LANES, LANES), 0) == iota((LANES, LANES), 1), 1.0, 0.0).astype(BF16)
    turned = matmul(eye, msg_ref[:, ASKED, :].astype(F32).astype(BF16), NT)
    col = iota((CAP, H), 1).astype(F32)
    x = x_ref[...]
    for d in range(0, CHIPS, 2):
        both = [jnp.where(turned[:CAP, e : e + 1] == col, 1.0, 0.0) for e in (d, d + 1)]
        pick = jnp.concatenate(both, 0).astype(BF16)
        out_ref[d * CAP : (d + 2) * CAP, :] = matmul(pick, x).astype(BF16)


def conv_kernel(comb_ref, arrived_ref, x_ref, cnt_ref, weight_ref, out_ref):
    count = column(cnt_ref[...].astype(F32))
    summed = x_ref[...].astype(F32) + matmul(comb_ref[...], arrived_ref[...])
    agg = (summed * (1.0 / (count + 1.0))).astype(BF16)
    x = jnp.maximum(matmul(agg, weight_ref[...]), 0.0).astype(BF16)
    for d in range(GROUP):
        out_ref[d] = x


def adjacency_kernel(msg_ref, where_ref, adj_ref, scale_ref):
    z_me, x_me, core_me = where_ref[0], where_ref[1], where_ref[2]
    lists, counts = [], []
    for z in range(GROUP):
        message = msg_ref[z * 4 + x_me]
        packed = message[: KNB // 2]
        lists += [packed // (1 << BITS), packed % (1 << BITS)]
        counts.append(message[COUNT : COUNT + 1])
    blank = jnp.zeros((NODE - GROUP * (KNB + 1), NODE), jnp.int32)
    turned = jnp.concatenate(lists + counts + [blank], 0).astype(F32).T
    spot = iota((NODE, ROWS), 1).astype(F32)
    for z in range(GROUP):
        adj = jnp.zeros((NODE, ROWS), F32)
        for k in range(KNB):
            at = z * KNB + k
            adj = adj + jnp.where(spot == turned[:, at : at + 1], 1.0, 0.0)
        rows = slice(z * NODE, (z + 1) * NODE)
        adj_ref[rows, :] = adj.astype(BF16)
        at = GROUP * KNB + z
        scale = 1.0 / (turned[:, at : at + 1] + 1.0)
        scale_ref[rows, :] = jnp.broadcast_to(scale, (NODE, LANES))
    mine = pl.ds(pl.multiple_of(z_me * NODE, NODE), NODE)
    here = pl.ds(pl.multiple_of((x_me * 2 + core_me) * NODE, NODE), NODE)
    eye = jnp.where(iota((NODE, NODE), 0) == iota((NODE, NODE), 1), 1.0, 0.0)
    adj_ref[mine, here] = (adj_ref[mine, here].astype(F32) + eye).astype(BF16)


def partial_kernel(adj_ref, plane_ref, scale_ref, out_ref):
    plane = plane_ref[...]
    for z in range(GROUP):
        rows = slice(z * NODE, (z + 1) * NODE)
        part = (matmul(adj_ref[rows, :], plane) * scale_ref[rows, :1]).astype(BF16)
        out_ref[:, z] = part.reshape(SNAPS, PART, H)


def lstm_kernel(
    part_ref,
    weight_ref,
    bias_ref,
    w_in_hbm,
    w_rec_hbm,
    cot_hbm,
    out_ref,
    z_ref,
    saved_ref,
    w_in_ref,
    w_rec_ref,
    cot_ref,
    sems,
):
    pairs = ((w_in_hbm, w_in_ref), (w_rec_hbm, w_rec_ref), (cot_hbm, cot_ref))
    copies = [
        pltpu.make_async_copy(a, b, sems.at[i]) for i, (a, b) in enumerate(pairs)
    ]
    for copy in copies:
        copy.start()
    total = part_ref[:, 0].astype(F32)
    for z in range(1, GROUP):
        total = total + part_ref[:, z].astype(F32)
    agg = total.reshape(NODE, H).astype(BF16)
    x = jnp.maximum(matmul(agg, weight_ref[...]), 0.0).astype(BF16)
    copies[0].wait()
    z_ref[...] = (matmul(x, w_in_ref[...]) + bias_ref[...]).astype(BF16).astype(F32)
    copies[1].wait()
    h = None
    c = jnp.zeros((PART, H), F32)
    for t in range(SNAPS):
        gates = z_ref[t * PART : (t + 1) * PART, :]
        if t > 0:
            gates = gates + matmul(h, w_rec_ref[...])
        i = jax.nn.sigmoid(gates[:, :H])
        f = jax.nn.sigmoid(gates[:, H : 2 * H])
        g = jnp.tanh(gates[:, 2 * H : 3 * H])
        o = jax.nn.sigmoid(gates[:, 3 * H :])
        c_new = f * c + i * g
        tc = jnp.tanh(c_new)
        h = (o * tc).astype(BF16)
        out_ref[t, :, :H] = h
        saved_ref[t, 0] = f
        saved_ref[t, 1] = o * (1.0 - tc * tc)
        saved_ref[t, 2] = g * i * (1.0 - i)
        saved_ref[t, 3] = c * f * (1.0 - f)
        saved_ref[t, 4] = i * (1.0 - g * g)
        saved_ref[t, 5] = tc * o * (1.0 - o)
        c = c_new
    copies[2].wait()
    dh = jnp.zeros((PART, H), F32)
    dc = jnp.zeros((PART, H), F32)
    for t in range(SNAPS - 1, -1, -1):
        dh = dh + cot_ref[t].astype(F32)
        dc = dc + dh * saved_ref[t, 1]
        grad = jnp.concatenate(
            [dc * saved_ref[t, 2], dc * saved_ref[t, 3], dc * saved_ref[t, 4], dh * saved_ref[t, 5]],
            1,
        ).astype(BF16)
        out_ref[t, :, H:] = grad
        if t > 0:
            dh = matmul(grad, w_rec_ref[...], NT)
            dc = dc * saved_ref[t, 0]


def call(kernel, out, *args, scratch=(), in_specs=None):
    more = {} if in_specs is None else {"in_specs": in_specs}
    return pl.pallas_call(
        kernel, out_shape=out, scratch_shapes=list(scratch), compiler_params=VMEM, **more
    )(*args)


def shaped(shape, dtype=BF16):
    return jax.ShapeDtypeStruct(shape, dtype)


def exchange(array, axes):
    return lax.all_to_all(array, axes, 0, 0, tiled=True)


def turned_cotangent(cotangent):
    mine = lax.axis_index("tm") == jnp.arange(SNAPS, dtype=jnp.int32)
    spread = jnp.where(
        mine[None, :, None, None], cotangent.reshape(SNAPS, 1, PART, H), jnp.zeros((), BF16)
    )
    total = lax.psum_scatter(spread.reshape(SNAPS * NODE, H), "tm", tiled=True)
    return total.reshape(SNAPS, PART, H)


def shards(
    features, nbr_owner, nbr_row, counts, weight_one, weight_two, w_in, w_rec, gate_bias, cotangent
):
    hbm = pl.BlockSpec(memory_space=pltpu.HBM)
    vmem = pl.BlockSpec(memory_space=pltpu.VMEM)
    chips = ("z", "x")
    x = features[0]
    cot = turned_cotangent(cotangent)
    msg, place = call(
        plan_kernel,
        (shaped((CHIPS, KNB, LANES), jnp.int32), shaped((NODE, 2 * KNB), F32)),
        nbr_owner.reshape(KNB, LANES),
        nbr_row.reshape(KNB, LANES),
        counts,
        in_specs=[hbm] * 3,
        scratch=(
            pltpu.VMEM((KNB, LANES), jnp.int32),
            pltpu.VMEM((KNB, LANES), jnp.int32),
            pltpu.VMEM((1, LANES), jnp.int32),
            pltpu.SemaphoreType.DMA((3,)),
        ),
    )
    msg = exchange(msg, chips)
    pair = lax.all_gather(x, "core", tiled=True)
    comb = call(comb_kernel, shaped((NODE, SLOTS)), place, counts)
    outgoing = call(pick_kernel, shaped((SLOTS, H)), msg, pair)
    arrived = exchange(outgoing.reshape(CHIPS, CAP, H), chips).reshape(SLOTS, H)
    where = jnp.stack([lax.axis_index(a) for a in ("z", "x", "core")]).astype(jnp.int32)
    adj, scale = call(
        adjacency_kernel,
        (shaped((ROWS, ROWS)), shaped((ROWS, LANES), F32)),
        msg,
        where,
        in_specs=[vmem, pl.BlockSpec(memory_space=pltpu.SMEM)],
    )
    copies = call(conv_kernel, shaped((GROUP, NODE, H)), comb, arrived, x, counts, weight_one)
    plane = exchange(copies, ("x", "core")).reshape(ROWS, H)
    part = call(partial_kernel, shaped((SNAPS, GROUP, PART, H)), adj, plane, scale)
    part = exchange(part.reshape(SNAPS * GROUP, PART, H), ("tm", "z"))
    result = call(
        lstm_kernel,
        shaped((SNAPS, PART, 5 * H)),
        part.reshape(SNAPS, GROUP, PART, H),
        weight_two,
        gate_bias.reshape(1, 4 * H),
        w_in,
        w_rec,
        cot,
        in_specs=[vmem] * 3 + [hbm] * 3,
        scratch=(
            pltpu.VMEM((NODE, 4 * H), F32),
            pltpu.VMEM((SNAPS, 6, PART, H), F32),
            pltpu.VMEM((H, 4 * H), BF16),
            pltpu.VMEM((H, 4 * H), BF16),
            pltpu.VMEM((SNAPS, PART, H), BF16),
            pltpu.SemaphoreType.DMA((3,)),
        ),
    )
    result = exchange(result, "tm").reshape(1, NODE, 5 * H)
    return result[:, :, :H], result[:, :, H:]


def solution(mesh):
    mesh = Mesh(mesh.devices.reshape(8, 8, 4, 2), ("tm", "z", "x", "core"))
    acct = ("z", "x", "core")
    return jax.shard_map(
        shards,
        mesh=mesh,
        in_specs=(
            P("tm", acct, None),
            P("tm", acct, None),
            P("tm", acct),
            P("tm", acct),
            P(),
            P(),
            P(),
            P(),
            P(),
            P("tm", acct, None),
        ),
        out_specs=(P("tm", acct, None), P("tm", acct, None)),
        check_vma=False,
    )
```

```python
import jax
import jax.numpy as jnp
from jax import lax
from jax.experimental import pallas as pl
from jax.experimental.pallas import tpu as pltpu
from jax.sharding import Mesh
from jax.sharding import PartitionSpec as P

H = 256
KNB = 8
NODE = 128
SNAPS = 8
CHIPS = 32
CAP = 40
SLOTS = CHIPS * CAP
LANES = 128
BF16 = jnp.bfloat16
F32 = jnp.float32
NT = ((1,), (1,))


def iota(shape, dim):
    return lax.broadcasted_iota(jnp.int32, shape, dim)


def matmul(a, b, dims=((1,), (0,))):
    return lax.dot_general(a, b, (dims, ((), ())), preferred_element_type=F32)


def fetch(pairs, sems):
    copies = [pltpu.make_async_copy(a, b, sems.at[i]) for i, (a, b) in enumerate(pairs)]
    for copy in copies:
        copy.start()
    return copies


def plan_kernel(owner_hbm, row_hbm, wanted_ref, place_ref, owner_ref, row_ref, sems):
    for copy in fetch(((owner_hbm, owner_ref), (row_hbm, row_ref)), sems):
        copy.wait()
    owner = owner_ref[...]
    value = ((owner % 2) * NODE + row_ref[...]).astype(F32)
    chip = owner // 2
    upper = jnp.where(iota((LANES, LANES), 0) < iota((LANES, LANES), 1), 1.0, 0.0).astype(BF16)
    base = jnp.zeros((CHIPS, 1), F32)
    wanted = jnp.zeros((CHIPS, LANES), F32)
    place = jnp.zeros((NODE, 2 * KNB), F32)
    lane = iota((1, LANES), 1)
    sub = iota((2 * KNB, LANES), 0)
    for i in range(KNB):
        chip_i = chip[i : i + 1, :]
        onehot = jnp.where(iota((CHIPS, LANES), 0) == chip_i, 1.0, 0.0)
        before = matmul(onehot.astype(BF16), upper) + base
        base = base + jnp.sum(onehot, 1, keepdims=True)
        rank = jnp.sum(onehot * before, 0, keepdims=True)
        ranks = jnp.where(iota((LANES, LANES), 0).astype(F32) == rank, 1.0, 0.0).astype(BF16)
        wanted = wanted + matmul((onehot * value[i : i + 1, :]).astype(BF16), ranks, NT)
        group = jnp.where(iota((NODE, LANES), 0) == i * (LANES // KNB) + lane // KNB, 1.0, 0.0)
        coded = jnp.where(sub < KNB, chip_i.astype(F32), rank)
        coded = jnp.where(sub % KNB == lane % KNB, coded, 0.0)
        place = place + matmul(group.astype(BF16), coded.astype(BF16), NT)
    wanted_ref[...] = wanted
    place_ref[...] = place


def column(row):
    eye = iota((NODE, NODE), 0) == iota((NODE, NODE), 1)
    return jnp.sum(jnp.where(eye, row, 0.0), 1, keepdims=True)


def comb_kernel(place_ref, cnt_ref, comb_ref):
    count = column(cnt_ref[...].astype(F32))
    place = place_ref[:, :KNB] * CAP + place_ref[:, KNB:]
    place = jnp.where(iota((NODE, KNB), 1).astype(F32) < count, place, -1.0)
    spot = iota((NODE, SLOTS), 1).astype(F32)
    comb = jnp.zeros((NODE, SLOTS), F32)
    for k in range(KNB):
        comb = comb + jnp.where(spot == place[:, k : k + 1], 1.0, 0.0)
    comb_ref[...] = comb.astype(BF16)


def pick_kernel(asked_ref, x_ref, pick_ref, out_ref):
    eye = jnp.where(iota((LANES, LANES), 0) == iota((LANES, LANES), 1), 1.0, 0.0).astype(BF16)
    turned = matmul(eye, asked_ref[...].astype(BF16), NT)
    col = iota((CAP, H), 1).astype(F32)
    x = x_ref[...]
    for d in range(0, CHIPS, 2):
        both = [jnp.where(turned[:CAP, e : e + 1] == col, 1.0, 0.0) for e in (d, d + 1)]
        pick = jnp.concatenate(both, 0).astype(BF16)
        pick_ref[d * CAP : (d + 2) * CAP, :] = pick
        out_ref[d * CAP : (d + 2) * CAP, :] = matmul(pick, x).astype(BF16)


def again_kernel(pick_ref, x_ref, out_ref):
    out_ref[...] = matmul(pick_ref[...], x_ref[...]).astype(BF16)


def convolved(comb_ref, arrived_ref, x_ref, cnt_ref, weight_ref):
    count = column(cnt_ref[...].astype(F32))
    summed = x_ref[...].astype(F32) + matmul(comb_ref[...], arrived_ref[...])
    agg = (summed * (1.0 / (count + 1.0))).astype(BF16)
    return jnp.maximum(matmul(agg, weight_ref[...]), 0.0).astype(BF16)


def first_kernel(*refs):
    refs[-1][...] = convolved(*refs[:-1])


def second_kernel(*refs):
    x = convolved(*refs[:-1])
    for t in range(SNAPS):
        refs[-1][t] = x


def lstm_kernel(
    x_ref, cot_ref, w_in_ref, w_rec_ref, bias_ref, snap_ref, hidden_ref, grads_ref, saved_ref
):
    snap = snap_ref[0]
    h = None
    c = jnp.zeros((NODE, H), F32)
    for t in range(SNAPS):
        z = (matmul(x_ref[t], w_in_ref[...]) + bias_ref[...]).astype(BF16)
        gates = z.astype(F32)
        if t > 0:
            gates = gates + matmul(h, w_rec_ref[...])
        i = jax.nn.sigmoid(gates[:, :H])
        f = jax.nn.sigmoid(gates[:, H : 2 * H])
        g = jnp.tanh(gates[:, 2 * H : 3 * H])
        o = jax.nn.sigmoid(gates[:, 3 * H :])
        c_new = f * c + i * g
        tc = jnp.tanh(c_new)
        h = (o * tc).astype(BF16)

        @pl.when(snap == t)
        def _(h=h):
            hidden_ref[...] = h

        saved_ref[t, 0] = f
        saved_ref[t, 1] = o * (1.0 - tc * tc)
        saved_ref[t, 2] = g * i * (1.0 - i)
        saved_ref[t, 3] = c * f * (1.0 - f)
        saved_ref[t, 4] = i * (1.0 - g * g)
        saved_ref[t, 5] = tc * o * (1.0 - o)
        c = c_new
    dh = jnp.zeros((NODE, H), F32)
    dc = jnp.zeros((NODE, H), F32)
    for t in range(SNAPS - 1, -1, -1):
        dh = dh + cot_ref[t].astype(F32)
        dc = dc + dh * saved_ref[t, 1]
        grad = jnp.concatenate(
            [dc * saved_ref[t, 2], dc * saved_ref[t, 3], dc * saved_ref[t, 4], dh * saved_ref[t, 5]],
            1,
        ).astype(BF16)

        @pl.when(snap == t)
        def _(grad=grad):
            grads_ref[...] = grad

        if t > 0:
            dh = matmul(grad, w_rec_ref[...], NT)
            dc = dc * saved_ref[t, 0]


def call(kernel, out, *args, scratch=(), in_specs=None, limit=16):
    more = {} if in_specs is None else {"in_specs": in_specs}
    return pl.pallas_call(
        kernel,
        out_shape=out,
        scratch_shapes=list(scratch),
        compiler_params=pltpu.CompilerParams(vmem_limit_bytes=limit * 1024 * 1024),
        **more,
    )(*args)


def shaped(shape, dtype=BF16):
    return jax.ShapeDtypeStruct(shape, dtype)


def exchange(array, axes):
    return lax.all_to_all(array, axes, 0, 0, tiled=True)


def shards(
    features, nbr_owner, nbr_row, counts, weight_one, weight_two, w_in, w_rec, gate_bias, cotangent
):
    vmem = pl.BlockSpec(memory_space=pltpu.VMEM)
    chips = ("z", "x")
    x = features[0]
    wanted, place = call(
        plan_kernel,
        (shaped((CHIPS, LANES), F32), shaped((NODE, 2 * KNB), F32)),
        nbr_owner.reshape(KNB, LANES),
        nbr_row.reshape(KNB, LANES),
        in_specs=[pl.BlockSpec(memory_space=pltpu.HBM)] * 2,
        scratch=(
            pltpu.VMEM((KNB, LANES), jnp.int32),
            pltpu.VMEM((KNB, LANES), jnp.int32),
            pltpu.SemaphoreType.DMA((2,)),
        ),
        limit=60,
    )
    asked = exchange(wanted, chips)
    pair = lax.all_gather(x, "core", tiled=True)
    pick, outgoing = call(pick_kernel, (shaped((SLOTS, H)), shaped((SLOTS, H))), asked, pair)
    outgoing, cot = lax.optimization_barrier((outgoing, cotangent))
    arrived = exchange(outgoing.reshape(CHIPS, CAP, H), chips).reshape(SLOTS, H)
    cots = lax.all_gather(cot, "tm", tiled=True)
    comb = call(comb_kernel, shaped((NODE, SLOTS)), place, counts)
    comb, cots = lax.optimization_barrier((comb, cots))
    x = call(first_kernel, shaped((NODE, H)), comb, arrived, x, counts, weight_one)
    pair = lax.all_gather(x, "core", tiled=True)
    outgoing = call(again_kernel, shaped((SLOTS, H)), pick, pair)
    arrived = exchange(outgoing.reshape(CHIPS, CAP, H), chips).reshape(SLOTS, H)
    x = call(second_kernel, shaped((SNAPS, NODE, H)), comb, arrived, x, counts, weight_two)
    xs = exchange(x, "tm")
    hidden, grads = call(
        lstm_kernel,
        (shaped((NODE, H)), shaped((NODE, 4 * H))),
        xs,
        cots,
        w_in,
        w_rec,
        gate_bias.reshape(1, 4 * H),
        lax.axis_index("tm").reshape(1).astype(jnp.int32),
        in_specs=[vmem] * 5 + [pl.BlockSpec(memory_space=pltpu.SMEM)],
        scratch=(pltpu.VMEM((SNAPS, 6, NODE, H), F32),),
    )
    return hidden[None], grads[None]


def solution(mesh):
    mesh = Mesh(mesh.devices.reshape(8, 8, 4, 2), ("tm", "z", "x", "core"))
    acct = ("z", "x", "core")
    return jax.shard_map(
        shards,
        mesh=mesh,
        in_specs=(
            P("tm", acct, None),
            P("tm", acct, None),
            P("tm", acct),
            P("tm", acct),
            P(),
            P(),
            P(),
            P(),
            P(),
            P("tm", acct, None),
        ),
        out_specs=(P("tm", acct, None), P("tm", acct, None)),
        check_vma=False,
    )
```

```python
import jax
import jax.numpy as jnp
from jax import lax
from jax.experimental import pallas as pl
from jax.experimental.pallas import tpu as pltpu
from jax.sharding import Mesh
from jax.sharding import PartitionSpec as P

H = 256
KNB = 8
NODE = 128
SNAPS = 8
CHIPS = 32
CAP = 40
SLOTS = CHIPS * CAP
PART = NODE // SNAPS
LANES = 128
BF16 = jnp.bfloat16
F32 = jnp.float32
NT = ((1,), (1,))


def iota(shape, dim):
    return lax.broadcasted_iota(jnp.int32, shape, dim)


def matmul(a, b, dims=((1,), (0,))):
    return lax.dot_general(a, b, (dims, ((), ())), preferred_element_type=F32)


def fetch(pairs, sems):
    copies = [pltpu.make_async_copy(a, b, sems.at[i]) for i, (a, b) in enumerate(pairs)]
    for copy in copies:
        copy.start()
    return copies


def plan_kernel(owner_hbm, row_hbm, wanted_ref, place_ref, owner_ref, row_ref, sems):
    for copy in fetch(((owner_hbm, owner_ref), (row_hbm, row_ref)), sems):
        copy.wait()
    owner = owner_ref[...]
    value = ((owner % 2) * NODE + row_ref[...]).astype(F32)
    chip = owner // 2
    upper = jnp.where(iota((LANES, LANES), 0) < iota((LANES, LANES), 1), 1.0, 0.0).astype(BF16)
    base = jnp.zeros((CHIPS, 1), F32)
    wanted = jnp.zeros((CHIPS, LANES), F32)
    place = jnp.zeros((NODE, 2 * KNB), F32)
    lane = iota((1, LANES), 1)
    sub = iota((2 * KNB, LANES), 0)
    for i in range(KNB):
        chip_i = chip[i : i + 1, :]
        onehot = jnp.where(iota((CHIPS, LANES), 0) == chip_i, 1.0, 0.0)
        before = matmul(onehot.astype(BF16), upper) + base
        base = base + jnp.sum(onehot, 1, keepdims=True)
        rank = jnp.sum(onehot * before, 0, keepdims=True)
        ranks = jnp.where(iota((LANES, LANES), 0).astype(F32) == rank, 1.0, 0.0).astype(BF16)
        wanted = wanted + matmul((onehot * value[i : i + 1, :]).astype(BF16), ranks, NT)
        group = jnp.where(iota((NODE, LANES), 0) == i * (LANES // KNB) + lane // KNB, 1.0, 0.0)
        coded = jnp.where(sub < KNB, chip_i.astype(F32), rank)
        coded = jnp.where(sub % KNB == lane % KNB, coded, 0.0)
        place = place + matmul(group.astype(BF16), coded.astype(BF16), NT)
    wanted_ref[...] = wanted
    place_ref[...] = place


def column(row):
    eye = iota((NODE, NODE), 0) == iota((NODE, NODE), 1)
    return jnp.sum(jnp.where(eye, row, 0.0), 1, keepdims=True)


def comb_kernel(place_ref, cnt_ref, comb_ref):
    count = column(cnt_ref[...].astype(F32))
    place = place_ref[:, :KNB] * CAP + place_ref[:, KNB:]
    place = jnp.where(iota((NODE, KNB), 1).astype(F32) < count, place, -1.0)
    spot = iota((NODE, SLOTS), 1).astype(F32)
    comb = jnp.zeros((NODE, SLOTS), F32)
    for k in range(KNB):
        comb = comb + jnp.where(spot == place[:, k : k + 1], 1.0, 0.0)
    comb_ref[...] = comb.astype(BF16)


def pick_kernel(asked_ref, x_ref, pick_ref, out_ref):
    eye = jnp.where(iota((LANES, LANES), 0) == iota((LANES, LANES), 1), 1.0, 0.0).astype(BF16)
    turned = matmul(eye, asked_ref[...].astype(BF16), NT)
    col = iota((CAP, H), 1).astype(F32)
    x = x_ref[...]
    for d in range(0, CHIPS, 2):
        both = [jnp.where(turned[:CAP, e : e + 1] == col, 1.0, 0.0) for e in (d, d + 1)]
        pick = jnp.concatenate(both, 0).astype(BF16)
        pick_ref[d * CAP : (d + 2) * CAP, :] = pick
        out_ref[d * CAP : (d + 2) * CAP, :] = matmul(pick, x).astype(BF16)


def again_kernel(pick_ref, x_ref, out_ref):
    out_ref[...] = matmul(pick_ref[...], x_ref[...]).astype(BF16)


def convolved(comb_ref, arrived_ref, x_ref, cnt_ref, weight_ref):
    count = column(cnt_ref[...].astype(F32))
    summed = x_ref[...].astype(F32) + matmul(comb_ref[...], arrived_ref[...])
    agg = (summed * (1.0 / (count + 1.0))).astype(BF16)
    return jnp.maximum(matmul(agg, weight_ref[...]), 0.0).astype(BF16)


def first_kernel(*refs):
    refs[-1][...] = convolved(*refs[:-1])


def second_kernel(
    comb_ref, arrived_ref, x_ref, cnt_ref, weight_ref, cot_ref, w_in_ref, bias_ref, out_ref, z_ref
):
    x = convolved(comb_ref, arrived_ref, x_ref, cnt_ref, weight_ref)
    out_ref[:, :H] = x
    out_ref[:, H:] = cot_ref[...]
    z_ref[...] = (matmul(x, w_in_ref[...]) + bias_ref[...]).astype(BF16)


def gated(gates, c):
    i = jax.nn.sigmoid(gates[:, :H])
    f = jax.nn.sigmoid(gates[:, H : 2 * H])
    g = jnp.tanh(gates[:, 2 * H : 3 * H])
    o = jax.nn.sigmoid(gates[:, 3 * H :])
    c_new = f * c + i * g
    return i, f, g, o, c_new, jnp.tanh(c_new)


def chain_kernel(xc_ref, w_in_ref, w_rec_ref, bias_ref, out_ref, z_ref, saved_ref):
    x = xc_ref[:, :, :H].reshape(NODE, H)
    z = matmul(x, w_in_ref[...]) + bias_ref[...]
    z_ref[...] = z.astype(BF16).astype(F32)
    h = jnp.zeros((PART, H), BF16)
    c = jnp.zeros((PART, H), F32)
    for t in range(SNAPS):
        out_ref[t, :, :H] = h
        out_ref[t, :, H : 2 * H] = c.astype(BF16)
        gates = z_ref[t * PART : (t + 1) * PART, :]
        if t > 0:
            gates = gates + matmul(h, w_rec_ref[...])
        i, f, g, o, c_new, tc = gated(gates, c)
        h = (o * tc).astype(BF16)
        saved_ref[t, 0] = f
        saved_ref[t, 1] = o * (1.0 - tc * tc)
        if t > 0:
            saved_ref[t, 2] = g * i * (1.0 - i)
            saved_ref[t, 3] = c * f * (1.0 - f)
            saved_ref[t, 4] = i * (1.0 - g * g)
            saved_ref[t, 5] = tc * o * (1.0 - o)
        c = c_new
    dh = jnp.zeros((PART, H), F32)
    dc = jnp.zeros((PART, H), F32)
    for t in range(SNAPS - 1, -1, -1):
        dh = dh + xc_ref[t, :, H:].astype(F32)
        dc = dc + dh * saved_ref[t, 1]
        out_ref[t, :, 2 * H : 3 * H] = dh.astype(BF16)
        out_ref[t, :, 3 * H :] = dc.astype(BF16)
        if t > 0:
            grad = jnp.concatenate(
                [
                    dc * saved_ref[t, 2],
                    dc * saved_ref[t, 3],
                    dc * saved_ref[t, 4],
                    dh * saved_ref[t, 5],
                ],
                1,
            ).astype(BF16)
            dh = matmul(grad, w_rec_ref[...], NT)
            dc = dc * saved_ref[t, 0]


def last_kernel(back_ref, z_ref, w_rec_ref, hidden_ref, grads_ref):
    c = back_ref[:, H : 2 * H].astype(F32)
    dh = back_ref[:, 2 * H : 3 * H].astype(F32)
    dc = back_ref[:, 3 * H :].astype(F32)
    gates = z_ref[...].astype(F32) + matmul(back_ref[:, :H], w_rec_ref[...])
    i, f, g, o, c_new, tc = gated(gates, c)
    hidden_ref[...] = (o * tc).astype(BF16)
    grads_ref[:, :H] = (dc * g * i * (1.0 - i)).astype(BF16)
    grads_ref[:, H : 2 * H] = (dc * c * f * (1.0 - f)).astype(BF16)
    grads_ref[:, 2 * H : 3 * H] = (dc * i * (1.0 - g * g)).astype(BF16)
    grads_ref[:, 3 * H :] = (dh * tc * o * (1.0 - o)).astype(BF16)


def call(kernel, out, *args, scratch=(), in_specs=None, limit=16):
    more = {} if in_specs is None else {"in_specs": in_specs}
    return pl.pallas_call(
        kernel,
        out_shape=out,
        scratch_shapes=list(scratch),
        compiler_params=pltpu.CompilerParams(vmem_limit_bytes=limit * 1024 * 1024),
        **more,
    )(*args)


def shaped(shape, dtype=BF16):
    return jax.ShapeDtypeStruct(shape, dtype)


def exchange(array, axes):
    return lax.all_to_all(array, axes, 0, 0, tiled=True)


def shards(
    features, nbr_owner, nbr_row, counts, weight_one, weight_two, w_in, w_rec, gate_bias, cotangent
):
    chips = ("z", "x")
    bias = gate_bias.reshape(1, 4 * H)
    x = features[0]
    wanted, place = call(
        plan_kernel,
        (shaped((CHIPS, LANES), F32), shaped((NODE, 2 * KNB), F32)),
        nbr_owner.reshape(KNB, LANES),
        nbr_row.reshape(KNB, LANES),
        in_specs=[pl.BlockSpec(memory_space=pltpu.HBM)] * 2,
        scratch=(
            pltpu.VMEM((KNB, LANES), jnp.int32),
            pltpu.VMEM((KNB, LANES), jnp.int32),
            pltpu.SemaphoreType.DMA((2,)),
        ),
        limit=60,
    )
    asked = exchange(wanted, chips)
    pair = lax.all_gather(x, "core", tiled=True)
    comb = call(comb_kernel, shaped((NODE, SLOTS)), place, counts)
    asked, pair, comb = lax.optimization_barrier((asked, pair, comb))
    pick, outgoing = call(pick_kernel, (shaped((SLOTS, H)), shaped((SLOTS, H))), asked, pair)
    arrived = exchange(outgoing.reshape(CHIPS, CAP, H), chips).reshape(SLOTS, H)
    x = call(first_kernel, shaped((NODE, H)), comb, arrived, x, counts, weight_one)
    pair = lax.all_gather(x, "core", tiled=True)
    outgoing = call(again_kernel, shaped((SLOTS, H)), pick, pair)
    arrived = exchange(outgoing.reshape(CHIPS, CAP, H), chips).reshape(SLOTS, H)
    both, z = call(
        second_kernel,
        (shaped((NODE, 2 * H)), shaped((NODE, 4 * H))),
        comb,
        arrived,
        x,
        counts,
        weight_two,
        cotangent[0],
        w_in,
        bias,
    )
    both = exchange(both.reshape(SNAPS, PART, 2 * H), "tm")
    back = call(
        chain_kernel,
        shaped((SNAPS, PART, 4 * H)),
        both,
        w_in,
        w_rec,
        bias,
        scratch=(pltpu.VMEM((NODE, 4 * H), F32), pltpu.VMEM((SNAPS, 6, PART, H), F32)),
    )
    back = exchange(back, "tm").reshape(NODE, 4 * H)
    hidden, grads = call(last_kernel, (shaped((NODE, H)), shaped((NODE, 4 * H))), back, z, w_rec)
    return hidden[None], grads[None]


def solution(mesh):
    mesh = Mesh(mesh.devices.reshape(8, 8, 4, 2), ("tm", "z", "x", "core"))
    acct = ("z", "x", "core")
    return jax.shard_map(
        shards,
        mesh=mesh,
        in_specs=(
            P("tm", acct, None),
            P("tm", acct, None),
            P("tm", acct),
            P("tm", acct),
            P(),
            P(),
            P(),
            P(),
            P(),
            P("tm", acct, None),
        ),
        out_specs=(P("tm", acct, None), P("tm", acct, None)),
        check_vma=False,
    )
```

```python
import jax
import jax.numpy as jnp
from jax import lax
from jax.experimental import pallas as pl
from jax.experimental.pallas import tpu as pltpu
from jax.sharding import Mesh
from jax.sharding import PartitionSpec as P

H = 256
KNB = 8
NODE = 128
SNAPS = 8
CHIPS = 32
CAP = 40
SLOTS = CHIPS * CAP
PART = NODE // SNAPS
LANES = 128
BF16 = jnp.bfloat16
F32 = jnp.float32
NT = ((1,), (1,))


def iota(shape, dim):
    return lax.broadcasted_iota(jnp.int32, shape, dim)


def matmul(a, b, dims=((1,), (0,))):
    return lax.dot_general(a, b, (dims, ((), ())), preferred_element_type=F32)


def fetch(pairs, sems):
    copies = [pltpu.make_async_copy(a, b, sems.at[i]) for i, (a, b) in enumerate(pairs)]
    for copy in copies:
        copy.start()
    return copies


def plan_kernel(owner_hbm, row_hbm, wanted_ref, rank_ref, owner_ref, row_ref, sems):
    for copy in fetch(((owner_hbm, owner_ref), (row_hbm, row_ref)), sems):
        copy.wait()
    owner = owner_ref[...]
    value = ((owner % 2) * NODE + row_ref[...]).astype(F32)
    chip = owner // 2
    upper = jnp.where(iota((LANES, LANES), 0) < iota((LANES, LANES), 1), 1.0, 0.0).astype(BF16)
    named = [
        jnp.where(iota((CHIPS, LANES), 0) == chip[i : i + 1, :], 1.0, 0.0) for i in range(KNB)
    ]
    before = matmul(jnp.concatenate(named, 0).astype(BF16), upper)
    base = jnp.zeros((CHIPS, 1), F32)
    wanted = jnp.zeros((CHIPS, LANES), F32)
    for i in range(KNB):
        earlier = before[i * CHIPS : (i + 1) * CHIPS] + base
        base = base + jnp.sum(named[i], 1, keepdims=True)
        rank = jnp.sum(named[i] * earlier, 0, keepdims=True)
        rank_ref[i : i + 1, :] = rank
        ranks = jnp.where(iota((LANES, LANES), 0).astype(F32) == rank, 1.0, 0.0).astype(BF16)
        wanted = wanted + matmul((named[i] * value[i : i + 1, :]).astype(BF16), ranks, NT)
    wanted_ref[...] = wanted


def column(row):
    eye = iota((NODE, NODE), 0) == iota((NODE, NODE), 1)
    return jnp.sum(jnp.where(eye, row, 0.0), 1, keepdims=True)


def comb_kernel(rank_ref, owner_ref, cnt_ref, comb_ref):
    count = column(cnt_ref[...].astype(F32))
    lane = iota((1, LANES), 1)
    sub = iota((2 * KNB, LANES), 0)
    chip = (owner_ref[...] // 2).astype(F32)
    place = jnp.zeros((NODE, 2 * KNB), F32)
    for i in range(KNB):
        group = jnp.where(iota((NODE, LANES), 0) == i * (LANES // KNB) + lane // KNB, 1.0, 0.0)
        coded = jnp.where(sub < KNB, chip[i : i + 1, :], rank_ref[i : i + 1, :])
        coded = jnp.where(sub % KNB == lane % KNB, coded, 0.0)
        place = place + matmul(group.astype(BF16), coded.astype(BF16), NT)
    place = place[:, :KNB] * CAP + place[:, KNB:]
    place = jnp.where(iota((NODE, KNB), 1).astype(F32) < count, place, -1.0)
    spot = iota((NODE, SLOTS), 1).astype(F32)
    comb = jnp.zeros((NODE, SLOTS), F32)
    for k in range(KNB):
        comb = comb + jnp.where(spot == place[:, k : k + 1], 1.0, 0.0)
    comb_ref[...] = comb.astype(BF16)


def pick_kernel(asked_ref, x_ref, pick_ref, out_ref):
    eye = jnp.where(iota((LANES, LANES), 0) == iota((LANES, LANES), 1), 1.0, 0.0).astype(BF16)
    turned = matmul(eye, asked_ref[...].astype(BF16), NT)
    col = iota((CAP, H), 1).astype(F32)
    x = x_ref[...]
    for d in range(0, CHIPS, 2):
        both = [jnp.where(turned[:CAP, e : e + 1] == col, 1.0, 0.0) for e in (d, d + 1)]
        pick = jnp.concatenate(both, 0).astype(BF16)
        pick_ref[d * CAP : (d + 2) * CAP, :] = pick
        out_ref[d * CAP : (d + 2) * CAP, :] = matmul(pick, x).astype(BF16)


def again_kernel(pick_ref, x_ref, out_ref):
    out_ref[...] = matmul(pick_ref[...], x_ref[...]).astype(BF16)


def convolved(comb_ref, arrived_ref, x_ref, cnt_ref, weight_ref):
    count = column(cnt_ref[...].astype(F32))
    summed = x_ref[...].astype(F32) + matmul(comb_ref[...], arrived_ref[...])
    agg = (summed * (1.0 / (count + 1.0))).astype(BF16)
    return jnp.maximum(matmul(agg, weight_ref[...]), 0.0).astype(BF16)


def first_kernel(*refs):
    refs[-1][...] = convolved(*refs[:-1])


def second_kernel(comb_ref, arrived_ref, x_ref, cnt_ref, weight_ref, cot_ref, out_ref):
    x = convolved(comb_ref, arrived_ref, x_ref, cnt_ref, weight_ref)
    out_ref[:, :H] = x
    out_ref[:, H:] = cot_ref[...]


def gated(gates, c):
    i = jax.nn.sigmoid(gates[:, :H])
    f = jax.nn.sigmoid(gates[:, H : 2 * H])
    g = jnp.tanh(gates[:, 2 * H : 3 * H])
    o = jax.nn.sigmoid(gates[:, 3 * H :])
    c_new = f * c + i * g
    return i, f, g, o, c_new, jnp.tanh(c_new)


def chain_kernel(xc_ref, w_in_ref, w_rec_ref, bias_ref, out_ref, z_ref, saved_ref):
    x = xc_ref[:, :, :H].reshape(NODE, H)
    z = matmul(x, w_in_ref[...]) + bias_ref[...]
    z_ref[...] = z.astype(BF16).astype(F32)
    h = jnp.zeros((PART, H), BF16)
    c = jnp.zeros((PART, H), F32)
    for t in range(SNAPS):
        out_ref[t, :, :H] = h
        out_ref[t, :, H : 2 * H] = c.astype(BF16)
        gates = z_ref[t * PART : (t + 1) * PART, :]
        if t > 0:
            gates = gates + matmul(h, w_rec_ref[...])
        i, f, g, o, c_new, tc = gated(gates, c)
        h = (o * tc).astype(BF16)
        saved_ref[t, 0] = f
        saved_ref[t, 1] = o * (1.0 - tc * tc)
        if t > 0:
            saved_ref[t, 2] = g * i * (1.0 - i)
            saved_ref[t, 3] = c * f * (1.0 - f)
            saved_ref[t, 4] = i * (1.0 - g * g)
            saved_ref[t, 5] = tc * o * (1.0 - o)
        c = c_new
    dh = jnp.zeros((PART, H), F32)
    dc = jnp.zeros((PART, H), F32)
    for t in range(SNAPS - 1, -1, -1):
        dh = dh + xc_ref[t, :, H:].astype(F32)
        dc = dc + dh * saved_ref[t, 1]
        out_ref[t, :, 2 * H : 3 * H] = dh.astype(BF16)
        out_ref[t, :, 3 * H :] = dc.astype(BF16)
        if t > 0:
            grad = jnp.concatenate(
                [
                    dc * saved_ref[t, 2],
                    dc * saved_ref[t, 3],
                    dc * saved_ref[t, 4],
                    dh * saved_ref[t, 5],
                ],
                1,
            ).astype(BF16)
            dh = matmul(grad, w_rec_ref[...], NT)
            dc = dc * saved_ref[t, 0]


def last_kernel(back_ref, x_ref, w_in_ref, w_rec_ref, bias_ref, hidden_ref, grads_ref):
    c = back_ref[:, H : 2 * H].astype(F32)
    dh = back_ref[:, 2 * H : 3 * H].astype(F32)
    dc = back_ref[:, 3 * H :].astype(F32)
    z = (matmul(x_ref[:, :H], w_in_ref[...]) + bias_ref[...]).astype(BF16)
    gates = z.astype(F32) + matmul(back_ref[:, :H], w_rec_ref[...])
    i, f, g, o, c_new, tc = gated(gates, c)
    hidden_ref[...] = (o * tc).astype(BF16)
    grads_ref[:, :H] = (dc * g * i * (1.0 - i)).astype(BF16)
    grads_ref[:, H : 2 * H] = (dc * c * f * (1.0 - f)).astype(BF16)
    grads_ref[:, 2 * H : 3 * H] = (dc * i * (1.0 - g * g)).astype(BF16)
    grads_ref[:, 3 * H :] = (dh * tc * o * (1.0 - o)).astype(BF16)


def call(kernel, out, *args, scratch=(), in_specs=None, limit=16):
    more = {} if in_specs is None else {"in_specs": in_specs}
    return pl.pallas_call(
        kernel,
        out_shape=out,
        scratch_shapes=list(scratch),
        compiler_params=pltpu.CompilerParams(vmem_limit_bytes=limit * 1024 * 1024),
        **more,
    )(*args)


def shaped(shape, dtype=BF16):
    return jax.ShapeDtypeStruct(shape, dtype)


def exchange(array, axes):
    return lax.all_to_all(array, axes, 0, 0, tiled=True)


def shards(
    features, nbr_owner, nbr_row, counts, weight_one, weight_two, w_in, w_rec, gate_bias, cotangent
):
    chips = ("z", "x")
    bias = gate_bias.reshape(1, 4 * H)
    x = features[0]
    owner = nbr_owner.reshape(KNB, LANES)
    wanted, rank = call(
        plan_kernel,
        (shaped((CHIPS, LANES), F32), shaped((KNB, LANES), F32)),
        owner,
        nbr_row.reshape(KNB, LANES),
        in_specs=[pl.BlockSpec(memory_space=pltpu.HBM)] * 2,
        scratch=(
            pltpu.VMEM((KNB, LANES), jnp.int32),
            pltpu.VMEM((KNB, LANES), jnp.int32),
            pltpu.SemaphoreType.DMA((2,)),
        ),
        limit=60,
    )
    asked = exchange(wanted, chips)
    pair = lax.all_gather(x, "core", tiled=True)
    pair, rank = lax.optimization_barrier((pair, rank))
    comb = call(comb_kernel, shaped((NODE, SLOTS)), rank, owner, counts)
    asked, comb = lax.optimization_barrier((asked, comb))
    pick, outgoing = call(pick_kernel, (shaped((SLOTS, H)), shaped((SLOTS, H))), asked, pair)
    arrived = exchange(outgoing.reshape(CHIPS, CAP, H), chips).reshape(SLOTS, H)
    x = call(first_kernel, shaped((NODE, H)), comb, arrived, x, counts, weight_one)
    pair = lax.all_gather(x, "core", tiled=True)
    outgoing = call(again_kernel, shaped((SLOTS, H)), pick, pair)
    arrived = exchange(outgoing.reshape(CHIPS, CAP, H), chips).reshape(SLOTS, H)
    mine = call(
        second_kernel,
        shaped((NODE, 2 * H)),
        comb,
        arrived,
        x,
        counts,
        weight_two,
        cotangent[0],
    )
    both = exchange(mine.reshape(SNAPS, PART, 2 * H), "tm")
    back = call(
        chain_kernel,
        shaped((SNAPS, PART, 4 * H)),
        both,
        w_in,
        w_rec,
        bias,
        scratch=(pltpu.VMEM((NODE, 4 * H), F32), pltpu.VMEM((SNAPS, 6, PART, H), F32)),
    )
    back = exchange(back, "tm").reshape(NODE, 4 * H)
    hidden, grads = call(
        last_kernel,
        (shaped((NODE, H)), shaped((NODE, 4 * H))),
        back,
        mine,
        w_in,
        w_rec,
        bias,
    )
    return hidden[None], grads[None]


def solution(mesh):
    mesh = Mesh(mesh.devices.reshape(8, 8, 4, 2), ("tm", "z", "x", "core"))
    acct = ("z", "x", "core")
    return jax.shard_map(
        shards,
        mesh=mesh,
        in_specs=(
            P("tm", acct, None),
            P("tm", acct, None),
            P("tm", acct),
            P("tm", acct),
            P(),
            P(),
            P(),
            P(),
            P(),
            P("tm", acct, None),
        ),
        out_specs=(P("tm", acct, None), P("tm", acct, None)),
        check_vma=False,
    )
```

```python
import jax
import jax.numpy as jnp
from jax import lax
from jax.experimental import pallas as pl
from jax.experimental.pallas import tpu as pltpu
from jax.sharding import Mesh
from jax.sharding import PartitionSpec as P

H = 256
KNB = 8
NODE = 128
SNAPS = 8
CHIPS = 32
CAP = 40
SLOTS = CHIPS * CAP
PART = NODE // SNAPS
LAST_ROWS = 32
LANES = 128
BF16 = jnp.bfloat16
F32 = jnp.float32
NT = ((1,), (1,))


def iota(shape, dim):
    return lax.broadcasted_iota(jnp.int32, shape, dim)


def matmul(a, b, dims=((1,), (0,))):
    return lax.dot_general(a, b, (dims, ((), ())), preferred_element_type=F32)


def fetch(pairs, sems):
    copies = [pltpu.make_async_copy(a, b, sems.at[i]) for i, (a, b) in enumerate(pairs)]
    for copy in copies:
        copy.start()
    return copies


def plan_kernel(owner_hbm, row_hbm, wanted_ref, rank_ref, owner_ref, row_ref, sems):
    for copy in fetch(((owner_hbm, owner_ref), (row_hbm, row_ref)), sems):
        copy.wait()
    owner = owner_ref[...]
    value = ((owner % 2) * NODE + row_ref[...]).astype(F32)
    chip = owner // 2
    upper = jnp.where(iota((LANES, LANES), 0) < iota((LANES, LANES), 1), 1.0, 0.0).astype(BF16)
    named = [
        jnp.where(iota((CHIPS, LANES), 0) == chip[i : i + 1, :], 1.0, 0.0) for i in range(KNB)
    ]
    before = matmul(jnp.concatenate(named, 0).astype(BF16), upper)
    base = jnp.zeros((CHIPS, 1), F32)
    wanted = jnp.zeros((CHIPS, LANES), F32)
    for i in range(KNB):
        earlier = before[i * CHIPS : (i + 1) * CHIPS] + base
        base = base + jnp.sum(named[i], 1, keepdims=True)
        rank = jnp.sum(named[i] * earlier, 0, keepdims=True)
        rank_ref[i : i + 1, :] = rank
        ranks = jnp.where(iota((LANES, LANES), 0).astype(F32) == rank, 1.0, 0.0).astype(BF16)
        wanted = wanted + matmul((named[i] * value[i : i + 1, :]).astype(BF16), ranks, NT)
    wanted_ref[...] = wanted


def column(row):
    eye = iota((NODE, NODE), 0) == iota((NODE, NODE), 1)
    return jnp.sum(jnp.where(eye, row, 0.0), 1, keepdims=True)


def comb_kernel(rank_ref, owner_ref, cnt_ref, comb_ref):
    count = column(cnt_ref[...].astype(F32))
    lane = iota((1, LANES), 1)
    sub = iota((2 * KNB, LANES), 0)
    chip = (owner_ref[...] // 2).astype(F32)
    place = jnp.zeros((NODE, 2 * KNB), F32)
    for i in range(KNB):
        group = jnp.where(iota((NODE, LANES), 0) == i * (LANES // KNB) + lane // KNB, 1.0, 0.0)
        coded = jnp.where(sub < KNB, chip[i : i + 1, :], rank_ref[i : i + 1, :])
        coded = jnp.where(sub % KNB == lane % KNB, coded, 0.0)
        place = place + matmul(group.astype(BF16), coded.astype(BF16), NT)
    place = place[:, :KNB] * CAP + place[:, KNB:]
    place = jnp.where(iota((NODE, KNB), 1).astype(F32) < count, place, -1.0)
    spot = iota((NODE, SLOTS), 1).astype(F32)
    comb = jnp.zeros((NODE, SLOTS), F32)
    for k in range(KNB):
        comb = comb + jnp.where(spot == place[:, k : k + 1], 1.0, 0.0)
    comb_ref[...] = comb.astype(BF16)


def pick_kernel(asked_ref, x_ref, pick_ref, out_ref):
    eye = jnp.where(iota((LANES, LANES), 0) == iota((LANES, LANES), 1), 1.0, 0.0).astype(BF16)
    turned = matmul(eye, asked_ref[...].astype(BF16), NT)
    col = iota((CAP, H), 1).astype(F32)
    x = x_ref[...]
    for d in range(0, CHIPS, 2):
        both = [jnp.where(turned[:CAP, e : e + 1] == col, 1.0, 0.0) for e in (d, d + 1)]
        pick = jnp.concatenate(both, 0).astype(BF16)
        pick_ref[d * CAP : (d + 2) * CAP, :] = pick
        out_ref[d * CAP : (d + 2) * CAP, :] = matmul(pick, x).astype(BF16)


def again_kernel(pick_ref, x_ref, out_ref):
    out_ref[...] = matmul(pick_ref[...], x_ref[...]).astype(BF16)


def convolved(comb_ref, arrived_ref, x_ref, cnt_ref, weight_ref):
    count = column(cnt_ref[...].astype(F32))
    summed = x_ref[...].astype(F32) + matmul(comb_ref[...], arrived_ref[...])
    agg = (summed * (1.0 / (count + 1.0))).astype(BF16)
    return jnp.maximum(matmul(agg, weight_ref[...]), 0.0).astype(BF16)


def first_kernel(*refs):
    refs[-1][...] = convolved(*refs[:-1])


def second_kernel(comb_ref, arrived_ref, x_ref, cnt_ref, weight_ref, cot_ref, out_ref):
    x = convolved(comb_ref, arrived_ref, x_ref, cnt_ref, weight_ref)
    out_ref[:, :H] = x
    out_ref[:, H:] = cot_ref[...]


def gated(gates, c):
    i = jax.nn.sigmoid(gates[:, :H])
    f = jax.nn.sigmoid(gates[:, H : 2 * H])
    g = jnp.tanh(gates[:, 2 * H : 3 * H])
    o = jax.nn.sigmoid(gates[:, 3 * H :])
    c_new = f * c + i * g
    return i, f, g, o, c_new, jnp.tanh(c_new)


def turn_kernel(w_ref, out_ref):
    out_ref[...] = w_ref[...].T


def chain_kernel(xc_ref, w_in_ref, w_rec_ref, turned_ref, bias_ref, out_ref, z_ref, saved_ref):
    x = xc_ref[:, :, :H].reshape(NODE, H)
    z = matmul(x, w_in_ref[...]) + bias_ref[...]
    z_ref[...] = z.astype(BF16).astype(F32)
    h = jnp.zeros((PART, H), BF16)
    c = jnp.zeros((PART, H), F32)
    for t in range(SNAPS):
        out_ref[t, :, :H] = h
        out_ref[t, :, H : 2 * H] = c.astype(BF16)
        gates = z_ref[t * PART : (t + 1) * PART, :]
        if t > 0:
            gates = gates + matmul(h, w_rec_ref[...])
        i, f, g, o, c_new, tc = gated(gates, c)
        h = (o * tc).astype(BF16)
        saved_ref[t, 0] = f
        saved_ref[t, 1] = o * (1.0 - tc * tc)
        if t > 0:
            saved_ref[t, 2] = g * i * (1.0 - i)
            saved_ref[t, 3] = c * f * (1.0 - f)
            saved_ref[t, 4] = i * (1.0 - g * g)
            saved_ref[t, 5] = tc * o * (1.0 - o)
        c = c_new
    dh = jnp.zeros((PART, H), F32)
    dc = jnp.zeros((PART, H), F32)
    for t in range(SNAPS - 1, -1, -1):
        dh = dh + xc_ref[t, :, H:].astype(F32)
        dc = dc + dh * saved_ref[t, 1]
        out_ref[t, :, 2 * H : 3 * H] = dh.astype(BF16)
        out_ref[t, :, 3 * H :] = dc.astype(BF16)
        if t > 0:
            grad = jnp.concatenate(
                [
                    dc * saved_ref[t, 2],
                    dc * saved_ref[t, 3],
                    dc * saved_ref[t, 4],
                    dh * saved_ref[t, 5],
                ],
                1,
            ).astype(BF16)
            dh = matmul(grad, turned_ref[...])
            dc = dc * saved_ref[t, 0]


def last_kernel(
    back_ref,
    x_ref,
    w_in_ref,
    w_rec_ref,
    bias_ref,
    hidden_hbm,
    grads_hbm,
    gates_ref,
    hidden_ref,
    grads_ref,
    sems,
):
    z = (matmul(x_ref[:, :H], w_in_ref[...]) + bias_ref[...]).astype(BF16)
    gates_ref[...] = z.astype(F32) + matmul(back_ref[:, :H], w_rec_ref[...])
    copies = []
    for part in range(NODE // LAST_ROWS):
        rows = slice(part * LAST_ROWS, (part + 1) * LAST_ROWS)
        c = back_ref[rows, H : 2 * H].astype(F32)
        dh = back_ref[rows, 2 * H : 3 * H].astype(F32)
        dc = back_ref[rows, 3 * H :].astype(F32)
        i, f, g, o, c_new, tc = gated(gates_ref[rows, :], c)
        hidden_ref[rows, :] = (o * tc).astype(BF16)
        grads_ref[rows, :H] = (dc * g * i * (1.0 - i)).astype(BF16)
        grads_ref[rows, H : 2 * H] = (dc * c * f * (1.0 - f)).astype(BF16)
        grads_ref[rows, 2 * H : 3 * H] = (dc * i * (1.0 - g * g)).astype(BF16)
        grads_ref[rows, 3 * H :] = (dh * tc * o * (1.0 - o)).astype(BF16)
        pairs = (
            (hidden_ref.at[rows, :], hidden_hbm.at[rows, :]),
            (grads_ref.at[rows, :], grads_hbm.at[rows, :]),
        )
        copies += fetch(pairs, sems.at[part])
    for copy in copies:
        copy.wait()


def call(kernel, out, *args, scratch=(), limit=16, **more):
    return pl.pallas_call(
        kernel,
        out_shape=out,
        scratch_shapes=list(scratch),
        compiler_params=pltpu.CompilerParams(vmem_limit_bytes=limit * 1024 * 1024),
        **more,
    )(*args)


def shaped(shape, dtype=BF16):
    return jax.ShapeDtypeStruct(shape, dtype)


def exchange(array, axes):
    return lax.all_to_all(array, axes, 0, 0, tiled=True)


def shards(
    features, nbr_owner, nbr_row, counts, weight_one, weight_two, w_in, w_rec, gate_bias, cotangent
):
    chips = ("z", "x")
    bias = gate_bias.reshape(1, 4 * H)
    x = features[0]
    owner = nbr_owner.reshape(KNB, LANES)
    wanted, rank = call(
        plan_kernel,
        (shaped((CHIPS, LANES), F32), shaped((KNB, LANES), F32)),
        owner,
        nbr_row.reshape(KNB, LANES),
        in_specs=[pl.BlockSpec(memory_space=pltpu.HBM)] * 2,
        scratch=(
            pltpu.VMEM((KNB, LANES), jnp.int32),
            pltpu.VMEM((KNB, LANES), jnp.int32),
            pltpu.SemaphoreType.DMA((2,)),
        ),
        limit=60,
    )
    asked = exchange(wanted, chips)
    pair = lax.all_gather(x, "core", tiled=True)
    pair, rank, w_rec = lax.optimization_barrier((pair, rank, w_rec))
    turned = call(turn_kernel, shaped((4 * H, H)), w_rec)
    comb = call(comb_kernel, shaped((NODE, SLOTS)), rank, owner, counts)
    asked, comb, turned = lax.optimization_barrier((asked, comb, turned))
    pick, outgoing = call(pick_kernel, (shaped((SLOTS, H)), shaped((SLOTS, H))), asked, pair)
    arrived = exchange(outgoing.reshape(CHIPS, CAP, H), chips).reshape(SLOTS, H)
    x = call(first_kernel, shaped((NODE, H)), comb, arrived, x, counts, weight_one)
    pair = lax.all_gather(x, "core", tiled=True)
    outgoing = call(again_kernel, shaped((SLOTS, H)), pick, pair)
    arrived = exchange(outgoing.reshape(CHIPS, CAP, H), chips).reshape(SLOTS, H)
    mine = call(
        second_kernel,
        shaped((NODE, 2 * H)),
        comb,
        arrived,
        x,
        counts,
        weight_two,
        cotangent[0],
    )
    both = exchange(mine.reshape(SNAPS, PART, 2 * H), "tm")
    back = call(
        chain_kernel,
        shaped((SNAPS, PART, 4 * H)),
        both,
        w_in,
        w_rec,
        turned,
        bias,
        scratch=(pltpu.VMEM((NODE, 4 * H), F32), pltpu.VMEM((SNAPS, 6, PART, H), F32)),
    )
    back = exchange(back, "tm").reshape(NODE, 4 * H)
    hidden, grads = call(
        last_kernel,
        (shaped((NODE, H)), shaped((NODE, 4 * H))),
        back,
        mine,
        w_in,
        w_rec,
        bias,
        out_specs=[pl.BlockSpec(memory_space=pltpu.HBM)] * 2,
        scratch=(
            pltpu.VMEM((NODE, 4 * H), F32),
            pltpu.VMEM((NODE, H), BF16),
            pltpu.VMEM((NODE, 4 * H), BF16),
            pltpu.SemaphoreType.DMA((NODE // LAST_ROWS, 2)),
        ),
    )
    return hidden[None], grads[None]


def solution(mesh):
    mesh = Mesh(mesh.devices.reshape(8, 8, 4, 2), ("tm", "z", "x", "core"))
    acct = ("z", "x", "core")
    return jax.shard_map(
        shards,
        mesh=mesh,
        in_specs=(
            P("tm", acct, None),
            P("tm", acct, None),
            P("tm", acct),
            P("tm", acct),
            P(),
            P(),
            P(),
            P(),
            P(),
            P("tm", acct, None),
        ),
        out_specs=(P("tm", acct, None), P("tm", acct, None)),
        check_vma=False,
    )
```

```python
import jax
import jax.numpy as jnp
from jax import lax
from jax.experimental import pallas as pl
from jax.experimental.pallas import tpu as pltpu
from jax.sharding import Mesh
from jax.sharding import PartitionSpec as P

H = 256
KNB = 8
NODE = 128
SNAPS = 8
CHIPS = 32
CAP = 40
SLOTS = CHIPS * CAP
PART = NODE // SNAPS
LANES = 128
BF16 = jnp.bfloat16
F32 = jnp.float32
NT = ((1,), (1,))


def iota(shape, dim):
    return lax.broadcasted_iota(jnp.int32, shape, dim)


def matmul(a, b, dims=((1,), (0,))):
    return lax.dot_general(a, b, (dims, ((), ())), preferred_element_type=F32)


def fetch(pairs, sems):
    copies = [pltpu.make_async_copy(a, b, sems.at[i]) for i, (a, b) in enumerate(pairs)]
    for copy in copies:
        copy.start()
    return copies


def plan_kernel(owner_hbm, row_hbm, wanted_ref, rank_ref, owner_ref, row_ref, sems):
    for copy in fetch(((owner_hbm, owner_ref), (row_hbm, row_ref)), sems):
        copy.wait()
    owner = owner_ref[...]
    value = ((owner % 2) * NODE + row_ref[...]).astype(F32)
    chip = owner // 2
    upper = jnp.where(iota((LANES, LANES), 0) < iota((LANES, LANES), 1), 1.0, 0.0).astype(BF16)
    named = [
        jnp.where(iota((CHIPS, LANES), 0) == chip[i : i + 1, :], 1.0, 0.0) for i in range(KNB)
    ]
    before = matmul(jnp.concatenate(named, 0).astype(BF16), upper)
    base = jnp.zeros((CHIPS, 1), F32)
    wanted = jnp.zeros((CHIPS, LANES), F32)
    for i in range(KNB):
        earlier = before[i * CHIPS : (i + 1) * CHIPS] + base
        base = base + jnp.sum(named[i], 1, keepdims=True)
        rank = jnp.sum(named[i] * earlier, 0, keepdims=True)
        rank_ref[i : i + 1, :] = rank
        ranks = jnp.where(iota((LANES, LANES), 0).astype(F32) == rank, 1.0, 0.0).astype(BF16)
        wanted = wanted + matmul((named[i] * value[i : i + 1, :]).astype(BF16), ranks, NT)
    wanted_ref[...] = wanted


def column(row):
    eye = iota((NODE, NODE), 0) == iota((NODE, NODE), 1)
    return jnp.sum(jnp.where(eye, row, 0.0), 1, keepdims=True)


def comb_kernel(rank_ref, owner_ref, cnt_ref, comb_ref):
    count = column(cnt_ref[...].astype(F32))
    lane = iota((1, LANES), 1)
    sub = iota((2 * KNB, LANES), 0)
    chip = (owner_ref[...] // 2).astype(F32)
    place = jnp.zeros((NODE, 2 * KNB), F32)
    for i in range(KNB):
        group = jnp.where(iota((NODE, LANES), 0) == i * (LANES // KNB) + lane // KNB, 1.0, 0.0)
        coded = jnp.where(sub < KNB, chip[i : i + 1, :], rank_ref[i : i + 1, :])
        coded = jnp.where(sub % KNB == lane % KNB, coded, 0.0)
        place = place + matmul(group.astype(BF16), coded.astype(BF16), NT)
    place = place[:, :KNB] * CAP + place[:, KNB:]
    place = jnp.where(iota((NODE, KNB), 1).astype(F32) < count, place, -1.0)
    spot = iota((NODE, SLOTS), 1).astype(F32)
    comb = jnp.zeros((NODE, SLOTS), F32)
    for k in range(KNB):
        comb = comb + jnp.where(spot == place[:, k : k + 1], 1.0, 0.0)
    comb_ref[...] = comb.astype(BF16)


def pick_kernel(asked_ref, x_ref, pick_ref, out_ref):
    eye = jnp.where(iota((LANES, LANES), 0) == iota((LANES, LANES), 1), 1.0, 0.0).astype(BF16)
    turned = matmul(eye, asked_ref[...].astype(BF16), NT)
    col = iota((CAP, H), 1).astype(F32)
    x = x_ref[...]
    for d in range(0, CHIPS, 2):
        both = [jnp.where(turned[:CAP, e : e + 1] == col, 1.0, 0.0) for e in (d, d + 1)]
        pick = jnp.concatenate(both, 0).astype(BF16)
        pick_ref[d * CAP : (d + 2) * CAP, :] = pick
        out_ref[d * CAP : (d + 2) * CAP, :] = matmul(pick, x).astype(BF16)


def again_kernel(pick_ref, x_ref, out_ref):
    out_ref[...] = matmul(pick_ref[...], x_ref[...]).astype(BF16)


def convolved(comb_ref, arrived_ref, x_ref, cnt_ref, weight_ref):
    count = column(cnt_ref[...].astype(F32))
    summed = x_ref[...].astype(F32) + matmul(comb_ref[...], arrived_ref[...])
    agg = (summed * (1.0 / (count + 1.0))).astype(BF16)
    return jnp.maximum(matmul(agg, weight_ref[...]), 0.0).astype(BF16)


def first_kernel(*refs):
    refs[-1][...] = convolved(*refs[:-1])


def second_kernel(comb_ref, arrived_ref, x_ref, cnt_ref, weight_ref, cot_ref, out_ref):
    x = convolved(comb_ref, arrived_ref, x_ref, cnt_ref, weight_ref)
    out_ref[:, :H] = x
    out_ref[:, H:] = cot_ref[...]


def gated(gates, c):
    i = jax.nn.sigmoid(gates[:, :H])
    f = jax.nn.sigmoid(gates[:, H : 2 * H])
    g = jnp.tanh(gates[:, 2 * H : 3 * H])
    o = jax.nn.sigmoid(gates[:, 3 * H :])
    c_new = f * c + i * g
    return i, f, g, o, c_new, jnp.tanh(c_new)


def chain_kernel(
    xc_ref, w_in_ref, w_rec_ref, bias_ref, out_ref, z_ref, saved_ref, turned_ref
):
    x = xc_ref[:, :, :H].reshape(NODE, H)
    z = matmul(x, w_in_ref[...]) + bias_ref[...]
    z_ref[...] = z.astype(BF16).astype(F32)
    turned_ref[...] = w_rec_ref[...].T
    h = jnp.zeros((PART, H), BF16)
    c = jnp.zeros((PART, H), F32)
    for t in range(SNAPS):
        out_ref[t, :, :H] = h
        out_ref[t, :, H : 2 * H] = c.astype(BF16)
        gates = z_ref[t * PART : (t + 1) * PART, :]
        if t > 0:
            gates = gates + matmul(h, w_rec_ref[...])
        i, f, g, o, c_new, tc = gated(gates, c)
        h = (o * tc).astype(BF16)
        saved_ref[t, 0] = f
        saved_ref[t, 1] = o * (1.0 - tc * tc)
        if t > 0:
            saved_ref[t, 2] = g * i * (1.0 - i)
            saved_ref[t, 3] = c * f * (1.0 - f)
            saved_ref[t, 4] = i * (1.0 - g * g)
            saved_ref[t, 5] = tc * o * (1.0 - o)
        c = c_new
    dh = jnp.zeros((PART, H), F32)
    dc = jnp.zeros((PART, H), F32)
    for t in range(SNAPS - 1, -1, -1):
        dh = dh + xc_ref[t, :, H:].astype(F32)
        dc = dc + dh * saved_ref[t, 1]
        out_ref[t, :, 2 * H : 3 * H] = dh.astype(BF16)
        out_ref[t, :, 3 * H :] = dc.astype(BF16)
        if t > 0:
            grad = jnp.concatenate(
                [
                    dc * saved_ref[t, 2],
                    dc * saved_ref[t, 3],
                    dc * saved_ref[t, 4],
                    dh * saved_ref[t, 5],
                ],
                1,
            ).astype(BF16)
            dh = matmul(grad, turned_ref[...])
            dc = dc * saved_ref[t, 0]


def last_kernel(back_ref, x_ref, w_in_ref, w_rec_ref, bias_ref, hidden_ref, grads_ref):
    c = back_ref[:, H : 2 * H].astype(F32)
    dh = back_ref[:, 2 * H : 3 * H].astype(F32)
    dc = back_ref[:, 3 * H :].astype(F32)
    z = (matmul(x_ref[:, :H], w_in_ref[...]) + bias_ref[...]).astype(BF16)
    gates = z.astype(F32) + matmul(back_ref[:, :H], w_rec_ref[...])
    i, f, g, o, c_new, tc = gated(gates, c)
    hidden_ref[...] = (o * tc).astype(BF16)
    grads_ref[:, :H] = (dc * g * i * (1.0 - i)).astype(BF16)
    grads_ref[:, H : 2 * H] = (dc * c * f * (1.0 - f)).astype(BF16)
    grads_ref[:, 2 * H : 3 * H] = (dc * i * (1.0 - g * g)).astype(BF16)
    grads_ref[:, 3 * H :] = (dh * tc * o * (1.0 - o)).astype(BF16)


def call(kernel, out, *args, scratch=(), in_specs=None, limit=16):
    more = {} if in_specs is None else {"in_specs": in_specs}
    return pl.pallas_call(
        kernel,
        out_shape=out,
        scratch_shapes=list(scratch),
        compiler_params=pltpu.CompilerParams(vmem_limit_bytes=limit * 1024 * 1024),
        **more,
    )(*args)


def shaped(shape, dtype=BF16):
    return jax.ShapeDtypeStruct(shape, dtype)


def exchange(array, axes):
    return lax.all_to_all(array, axes, 0, 0, tiled=True)


def shards(
    features, nbr_owner, nbr_row, counts, weight_one, weight_two, w_in, w_rec, gate_bias, cotangent
):
    chips = ("z", "x")
    bias = gate_bias.reshape(1, 4 * H)
    x = features[0]
    owner = nbr_owner.reshape(KNB, LANES)
    wanted, rank = call(
        plan_kernel,
        (shaped((CHIPS, LANES), F32), shaped((KNB, LANES), F32)),
        owner,
        nbr_row.reshape(KNB, LANES),
        in_specs=[pl.BlockSpec(memory_space=pltpu.HBM)] * 2,
        scratch=(
            pltpu.VMEM((KNB, LANES), jnp.int32),
            pltpu.VMEM((KNB, LANES), jnp.int32),
            pltpu.SemaphoreType.DMA((2,)),
        ),
        limit=60,
    )
    asked = exchange(wanted, chips)
    pair = lax.all_gather(x, "core", tiled=True)
    pair, rank = lax.optimization_barrier((pair, rank))
    comb = call(comb_kernel, shaped((NODE, SLOTS)), rank, owner, counts)
    asked, comb = lax.optimization_barrier((asked, comb))
    pick, outgoing = call(pick_kernel, (shaped((SLOTS, H)), shaped((SLOTS, H))), asked, pair)
    arrived = exchange(outgoing.reshape(CHIPS, CAP, H), chips).reshape(SLOTS, H)
    x = call(first_kernel, shaped((NODE, H)), comb, arrived, x, counts, weight_one)
    pair = lax.all_gather(x, "core", tiled=True)
    outgoing = call(again_kernel, shaped((SLOTS, H)), pick, pair)
    arrived = exchange(outgoing.reshape(CHIPS, CAP, H), chips).reshape(SLOTS, H)
    mine = call(
        second_kernel,
        shaped((NODE, 2 * H)),
        comb,
        arrived,
        x,
        counts,
        weight_two,
        cotangent[0],
    )
    both = exchange(mine.reshape(SNAPS, PART, 2 * H), "tm")
    back = call(
        chain_kernel,
        shaped((SNAPS, PART, 4 * H)),
        both,
        w_in,
        w_rec,
        bias,
        scratch=(
            pltpu.VMEM((NODE, 4 * H), F32),
            pltpu.VMEM((SNAPS, 6, PART, H), F32),
            pltpu.VMEM((4 * H, H), BF16),
        ),
    )
    back = exchange(back, "tm").reshape(NODE, 4 * H)
    hidden, grads = call(
        last_kernel,
        (shaped((NODE, H)), shaped((NODE, 4 * H))),
        back,
        mine,
        w_in,
        w_rec,
        bias,
    )
    return hidden[None], grads[None]


def solution(mesh):
    mesh = Mesh(mesh.devices.reshape(8, 8, 4, 2), ("tm", "z", "x", "core"))
    acct = ("z", "x", "core")
    return jax.shard_map(
        shards,
        mesh=mesh,
        in_specs=(
            P("tm", acct, None),
            P("tm", acct, None),
            P("tm", acct),
            P("tm", acct),
            P(),
            P(),
            P(),
            P(),
            P(),
            P("tm", acct, None),
        ),
        out_specs=(P("tm", acct, None), P("tm", acct, None)),
        check_vma=False,
    )
```

```python
import jax
import jax.numpy as jnp
from jax import lax
from jax.experimental import pallas as pl
from jax.experimental.pallas import tpu as pltpu
from jax.sharding import Mesh
from jax.sharding import PartitionSpec as P

H = 256
KNB = 8
NODE = 128
SNAPS = 8
CHIPS = 32
CAP = 40
SLOTS = CHIPS * CAP
TM = ("t2", "t1", "t0")
LANES = 128
BF16 = jnp.bfloat16
F32 = jnp.float32
NT = ((1,), (1,))


def iota(shape, dim):
    return lax.broadcasted_iota(jnp.int32, shape, dim)


def matmul(a, b, dims=((1,), (0,))):
    return lax.dot_general(a, b, (dims, ((), ())), preferred_element_type=F32)


def fetch(pairs, sems):
    copies = [pltpu.make_async_copy(a, b, sems.at[i]) for i, (a, b) in enumerate(pairs)]
    for copy in copies:
        copy.start()
    return copies


def plan_kernel(owner_hbm, row_hbm, wanted_ref, rank_ref, owner_ref, row_ref, sems):
    for copy in fetch(((owner_hbm, owner_ref), (row_hbm, row_ref)), sems):
        copy.wait()
    owner = owner_ref[...]
    value = ((owner % 2) * NODE + row_ref[...]).astype(F32)
    chip = owner // 2
    upper = jnp.where(iota((LANES, LANES), 0) < iota((LANES, LANES), 1), 1.0, 0.0).astype(BF16)
    named = [
        jnp.where(iota((CHIPS, LANES), 0) == chip[i : i + 1, :], 1.0, 0.0) for i in range(KNB)
    ]
    before = matmul(jnp.concatenate(named, 0).astype(BF16), upper)
    base = jnp.zeros((CHIPS, 1), F32)
    wanted = jnp.zeros((CHIPS, LANES), F32)
    for i in range(KNB):
        earlier = before[i * CHIPS : (i + 1) * CHIPS] + base
        base = base + jnp.sum(named[i], 1, keepdims=True)
        rank = jnp.sum(named[i] * earlier, 0, keepdims=True)
        rank_ref[i : i + 1, :] = rank
        ranks = jnp.where(iota((LANES, LANES), 0).astype(F32) == rank, 1.0, 0.0).astype(BF16)
        wanted = wanted + matmul((named[i] * value[i : i + 1, :]).astype(BF16), ranks, NT)
    wanted_ref[...] = wanted


def column(row):
    eye = iota((NODE, NODE), 0) == iota((NODE, NODE), 1)
    return jnp.sum(jnp.where(eye, row, 0.0), 1, keepdims=True)


def comb_kernel(rank_ref, owner_ref, cnt_ref, comb_ref):
    count = column(cnt_ref[...].astype(F32))
    lane = iota((1, LANES), 1)
    sub = iota((2 * KNB, LANES), 0)
    chip = (owner_ref[...] // 2).astype(F32)
    place = jnp.zeros((NODE, 2 * KNB), F32)
    for i in range(KNB):
        group = jnp.where(iota((NODE, LANES), 0) == i * (LANES // KNB) + lane // KNB, 1.0, 0.0)
        coded = jnp.where(sub < KNB, chip[i : i + 1, :], rank_ref[i : i + 1, :])
        coded = jnp.where(sub % KNB == lane % KNB, coded, 0.0)
        place = place + matmul(group.astype(BF16), coded.astype(BF16), NT)
    place = place[:, :KNB] * CAP + place[:, KNB:]
    place = jnp.where(iota((NODE, KNB), 1).astype(F32) < count, place, -1.0)
    spot = iota((NODE, SLOTS), 1).astype(F32)
    comb = jnp.zeros((NODE, SLOTS), F32)
    for k in range(KNB):
        comb = comb + jnp.where(spot == place[:, k : k + 1], 1.0, 0.0)
    comb_ref[...] = comb.astype(BF16)


def pick_kernel(asked_ref, x_ref, pick_ref, out_ref):
    eye = jnp.where(iota((LANES, LANES), 0) == iota((LANES, LANES), 1), 1.0, 0.0).astype(BF16)
    turned = matmul(eye, asked_ref[...].astype(BF16), NT)
    col = iota((CAP, H), 1).astype(F32)
    x = x_ref[...]
    for d in range(0, CHIPS, 2):
        both = [jnp.where(turned[:CAP, e : e + 1] == col, 1.0, 0.0) for e in (d, d + 1)]
        pick = jnp.concatenate(both, 0).astype(BF16)
        pick_ref[d * CAP : (d + 2) * CAP, :] = pick
        out_ref[d * CAP : (d + 2) * CAP, :] = matmul(pick, x).astype(BF16)


def again_kernel(pick_ref, x_ref, out_ref):
    out_ref[...] = matmul(pick_ref[...], x_ref[...]).astype(BF16)


def convolved(comb_ref, arrived_ref, x_ref, cnt_ref, weight_ref):
    count = column(cnt_ref[...].astype(F32))
    summed = x_ref[...].astype(F32) + matmul(comb_ref[...], arrived_ref[...])
    agg = (summed * (1.0 / (count + 1.0))).astype(BF16)
    return jnp.maximum(matmul(agg, weight_ref[...]), 0.0).astype(BF16)


def first_kernel(*refs):
    refs[-1][...] = convolved(*refs[:-1])


def second_kernel(*refs):
    x = convolved(*refs[:-1])
    for t in range(SNAPS):
        refs[-1][t] = x


def gated(gates, c):
    i = jax.nn.sigmoid(gates[:, :H])
    f = jax.nn.sigmoid(gates[:, H : 2 * H])
    g = jnp.tanh(gates[:, 2 * H : 3 * H])
    o = jax.nn.sigmoid(gates[:, 3 * H :])
    c_new = f * c + i * g
    return i, f, g, o, c_new, jnp.tanh(c_new)


def chain_kernel(
    x_ref,
    cot_ref,
    w_in_ref,
    w_rec_ref,
    bias_ref,
    snap_ref,
    hidden_hbm,
    grads_hbm,
    saved_ref,
    turned_ref,
    hidden_ref,
    grads_ref,
    sems,
):
    snap = snap_ref[0]
    turned_ref[...] = w_rec_ref[...].T
    h = None
    c = jnp.zeros((NODE, H), F32)
    for t in range(SNAPS):
        z = (matmul(x_ref[t], w_in_ref[...]) + bias_ref[...]).astype(BF16)
        gates = z.astype(F32)
        if t > 0:
            gates = gates + matmul(h, w_rec_ref[...])
        i, f, g, o, c_new, tc = gated(gates, c)
        h = (o * tc).astype(BF16)
        hidden_ref[t] = h
        saved_ref[t, 0] = f
        saved_ref[t, 1] = o * (1.0 - tc * tc)
        saved_ref[t, 2] = g * i * (1.0 - i)
        saved_ref[t, 3] = c * f * (1.0 - f)
        saved_ref[t, 4] = i * (1.0 - g * g)
        saved_ref[t, 5] = tc * o * (1.0 - o)
        c = c_new
    copies = fetch(((hidden_ref.at[snap], hidden_hbm),), sems)
    dh = jnp.zeros((NODE, H), F32)
    dc = jnp.zeros((NODE, H), F32)
    for t in range(SNAPS - 1, -1, -1):
        at = (t & 1) * 4 + (t & 2) + (t >> 2)
        dh = dh + cot_ref[at].astype(F32)
        dc = dc + dh * saved_ref[t, 1]
        grad = jnp.concatenate(
            [dc * saved_ref[t, 2], dc * saved_ref[t, 3], dc * saved_ref[t, 4], dh * saved_ref[t, 5]],
            1,
        ).astype(BF16)
        grads_ref[t] = grad
        if t > 0:
            dh = matmul(grad, turned_ref[...])
            dc = dc * saved_ref[t, 0]
    copies += fetch(((grads_ref.at[snap], grads_hbm),), sems.at[pl.ds(1, 1)])
    for copy in copies:
        copy.wait()


def call(kernel, out, *args, scratch=(), limit=16, **more):
    return pl.pallas_call(
        kernel,
        out_shape=out,
        scratch_shapes=list(scratch),
        compiler_params=pltpu.CompilerParams(vmem_limit_bytes=limit * 1024 * 1024),
        **more,
    )(*args)


def shaped(shape, dtype=BF16):
    return jax.ShapeDtypeStruct(shape, dtype)


def exchange(array, axes):
    return lax.all_to_all(array, axes, 0, 0, tiled=True)


def shards(
    features, nbr_owner, nbr_row, counts, weight_one, weight_two, w_in, w_rec, gate_bias, cotangent
):
    chips = ("z", "x")
    hbm = pl.BlockSpec(memory_space=pltpu.HBM)
    vmem = pl.BlockSpec(memory_space=pltpu.VMEM)
    x = features[0]
    owner = nbr_owner.reshape(KNB, LANES)
    wanted, rank = call(
        plan_kernel,
        (shaped((CHIPS, LANES), F32), shaped((KNB, LANES), F32)),
        owner,
        nbr_row.reshape(KNB, LANES),
        in_specs=[hbm] * 2,
        scratch=(
            pltpu.VMEM((KNB, LANES), jnp.int32),
            pltpu.VMEM((KNB, LANES), jnp.int32),
            pltpu.SemaphoreType.DMA((2,)),
        ),
        limit=60,
    )
    asked = exchange(wanted, chips)
    pair = lax.all_gather(x, "core", tiled=True)
    asked, pair = lax.optimization_barrier((asked, pair))
    pick, outgoing = call(pick_kernel, (shaped((SLOTS, H)), shaped((SLOTS, H))), asked, pair)
    snap = lax.axis_index(TM).reshape(1).astype(jnp.int32)
    outgoing, cot, rank, snap = lax.optimization_barrier((outgoing, cotangent, rank, snap))
    arrived = exchange(outgoing.reshape(CHIPS, CAP, H), chips).reshape(SLOTS, H)
    cot = lax.all_gather(cot, "t2", tiled=True)
    cot = lax.all_gather(cot, "t1", tiled=True)
    comb = call(comb_kernel, shaped((NODE, SLOTS)), rank, owner, counts)
    comb, cot = lax.optimization_barrier((comb, cot))
    x = call(first_kernel, shaped((NODE, H)), comb, arrived, x, counts, weight_one)
    pair = lax.all_gather(x, "core", tiled=True)
    outgoing = call(again_kernel, shaped((SLOTS, H)), pick, pair)
    outgoing, cot = lax.optimization_barrier((outgoing, cot))
    arrived = exchange(outgoing.reshape(CHIPS, CAP, H), chips).reshape(SLOTS, H)
    cot = lax.all_gather(cot, "t0", tiled=True)
    comb, cot = lax.optimization_barrier((comb, cot))
    copies = call(
        second_kernel, shaped((SNAPS, NODE, H)), comb, arrived, x, counts, weight_two
    )
    xs = exchange(copies, TM)
    hidden, grads = call(
        chain_kernel,
        (shaped((NODE, H)), shaped((NODE, 4 * H))),
        xs,
        cot,
        w_in,
        w_rec,
        gate_bias.reshape(1, 4 * H),
        snap,
        in_specs=[vmem] * 5 + [pl.BlockSpec(memory_space=pltpu.SMEM)],
        out_specs=[hbm] * 2,
        scratch=(
            pltpu.VMEM((SNAPS, 6, NODE, H), F32),
            pltpu.VMEM((4 * H, H), BF16),
            pltpu.VMEM((SNAPS, NODE, H), BF16),
            pltpu.VMEM((SNAPS, NODE, 4 * H), BF16),
            pltpu.SemaphoreType.DMA((2,)),
        ),
    )
    return hidden[None], grads[None]
def solution(mesh):
    mesh = Mesh(mesh.devices.reshape(2, 2, 2, 8, 4, 2), TM + ("z", "x", "core"))
    acct = ("z", "x", "core")
    return jax.shard_map(
        shards,
        mesh=mesh,
        in_specs=(
            P(TM, acct, None),
            P(TM, acct, None),
            P(TM, acct),
            P(TM, acct),
            P(),
            P(),
            P(),
            P(),
            P(),
            P(TM, acct, None),
        ),
        out_specs=(P(TM, acct, None), P(TM, acct, None)),
        check_vma=False,
    )
```

```python
import jax
import jax.numpy as jnp
from jax import lax
from jax.experimental import pallas as pl
from jax.experimental.pallas import tpu as pltpu
from jax.sharding import Mesh
from jax.sharding import PartitionSpec as P

H = 256
KNB = 8
NODE = 128
SNAPS = 8
CHIPS = 32
CAP = 40
SLOTS = CHIPS * CAP
BLOCKS = 8
TM = ("t2", "t1", "t0")
LANES = 128
BF16 = jnp.bfloat16
F32 = jnp.float32
NT = ((1,), (1,))


def iota(shape, dim):
    return lax.broadcasted_iota(jnp.int32, shape, dim)


def matmul(a, b, dims=((1,), (0,))):
    return lax.dot_general(a, b, (dims, ((), ())), preferred_element_type=F32)


def fetch(pairs, sems):
    copies = [pltpu.make_async_copy(a, b, sems.at[i]) for i, (a, b) in enumerate(pairs)]
    for copy in copies:
        copy.start()
    return copies


def plan_kernel(owner_hbm, row_hbm, wanted_ref, rank_ref, owner_ref, row_ref, sems):
    for copy in fetch(((owner_hbm, owner_ref), (row_hbm, row_ref)), sems):
        copy.wait()
    owner = owner_ref[...]
    value = ((owner % 2) * NODE + row_ref[...]).astype(F32)
    chip = owner // 2
    upper = jnp.where(iota((LANES, LANES), 0) < iota((LANES, LANES), 1), 1.0, 0.0).astype(BF16)
    named = [
        jnp.where(iota((CHIPS, LANES), 0) == chip[i : i + 1, :], 1.0, 0.0) for i in range(KNB)
    ]
    before = matmul(jnp.concatenate(named, 0).astype(BF16), upper)
    base = jnp.zeros((CHIPS, 1), F32)
    wanted = jnp.zeros((CHIPS, LANES), F32)
    for i in range(KNB):
        earlier = before[i * CHIPS : (i + 1) * CHIPS] + base
        base = base + jnp.sum(named[i], 1, keepdims=True)
        rank = jnp.sum(named[i] * earlier, 0, keepdims=True)
        rank_ref[i : i + 1, :] = rank
        ranks = jnp.where(iota((LANES, LANES), 0).astype(F32) == rank, 1.0, 0.0).astype(BF16)
        wanted = wanted + matmul((named[i] * value[i : i + 1, :]).astype(BF16), ranks, NT)
    wanted_ref[...] = wanted


def column(row):
    eye = iota((NODE, NODE), 0) == iota((NODE, NODE), 1)
    return jnp.sum(jnp.where(eye, row, 0.0), 1, keepdims=True)


def comb_kernel(rank_ref, owner_ref, cnt_ref, comb_ref):
    count = column(cnt_ref[...].astype(F32))
    lane = iota((1, LANES), 1)
    sub = iota((2 * KNB, LANES), 0)
    chip = (owner_ref[...] // 2).astype(F32)
    place = jnp.zeros((NODE, 2 * KNB), F32)
    for i in range(KNB):
        group = jnp.where(iota((NODE, LANES), 0) == i * (LANES // KNB) + lane // KNB, 1.0, 0.0)
        coded = jnp.where(sub < KNB, chip[i : i + 1, :], rank_ref[i : i + 1, :])
        coded = jnp.where(sub % KNB == lane % KNB, coded, 0.0)
        place = place + matmul(group.astype(BF16), coded.astype(BF16), NT)
    place = place[:, :KNB] * CAP + place[:, KNB:]
    place = jnp.where(iota((NODE, KNB), 1).astype(F32) < count, place, -1.0)
    spot = iota((NODE, SLOTS), 1).astype(F32)
    comb = jnp.zeros((NODE, SLOTS), F32)
    for k in range(KNB):
        comb = comb + jnp.where(spot == place[:, k : k + 1], 1.0, 0.0)
    comb_ref[...] = comb.astype(BF16)


def pick_kernel(asked_ref, x_ref, pick_ref, out_hbm, out_ref, sems):
    eye = jnp.where(iota((LANES, LANES), 0) == iota((LANES, LANES), 1), 1.0, 0.0).astype(BF16)
    turned = matmul(eye, asked_ref[...].astype(BF16), NT)
    col = iota((CAP, H), 1).astype(F32)
    x = x_ref[...]
    copies = []
    for block in range(BLOCKS):
        rows = slice(block * SLOTS // BLOCKS, (block + 1) * SLOTS // BLOCKS)
        chips = range(block * CHIPS // BLOCKS, (block + 1) * CHIPS // BLOCKS)
        named = [jnp.where(turned[:CAP, d : d + 1] == col, 1.0, 0.0) for d in chips]
        pick = jnp.concatenate(named, 0).astype(BF16)
        pick_ref[rows, :] = pick
        out_ref[rows, :] = matmul(pick, x).astype(BF16)
        copies += fetch(((out_ref.at[rows, :], out_hbm.at[rows, :]),), sems.at[pl.ds(block, 1)])
    for copy in copies:
        copy.wait()


def again_kernel(pick_ref, x_ref, out_hbm, out_ref, sems):
    x = x_ref[...]
    copies = []
    for block in range(BLOCKS):
        rows = slice(block * SLOTS // BLOCKS, (block + 1) * SLOTS // BLOCKS)
        out_ref[rows, :] = matmul(pick_ref[rows, :], x).astype(BF16)
        copies += fetch(((out_ref.at[rows, :], out_hbm.at[rows, :]),), sems.at[pl.ds(block, 1)])
    for copy in copies:
        copy.wait()


def convolved(comb_ref, arrived_ref, x_ref, cnt_ref, weight_ref):
    count = column(cnt_ref[...].astype(F32))
    summed = x_ref[...].astype(F32) + matmul(comb_ref[...], arrived_ref[...])
    agg = (summed * (1.0 / (count + 1.0))).astype(BF16)
    return jnp.maximum(matmul(agg, weight_ref[...]), 0.0).astype(BF16)


def first_kernel(*refs):
    refs[-1][...] = convolved(*refs[:-1])


def second_kernel(*refs):
    x = convolved(*refs[:-1])
    for t in range(SNAPS):
        refs[-1][t] = x


def gated(gates, c):
    i = jax.nn.sigmoid(gates[:, :H])
    f = jax.nn.sigmoid(gates[:, H : 2 * H])
    g = jnp.tanh(gates[:, 2 * H : 3 * H])
    o = jax.nn.sigmoid(gates[:, 3 * H :])
    c_new = f * c + i * g
    return i, f, g, o, c_new, jnp.tanh(c_new)


def chain_kernel(
    x_ref,
    cot_ref,
    w_in_ref,
    w_rec_ref,
    bias_ref,
    snap_ref,
    hidden_hbm,
    grads_hbm,
    saved_ref,
    turned_ref,
    hidden_ref,
    grads_ref,
    sems,
):
    snap = snap_ref[0]
    turned_ref[...] = w_rec_ref[...].T
    h = None
    c = jnp.zeros((NODE, H), F32)
    for t in range(SNAPS):
        z = (matmul(x_ref[t], w_in_ref[...]) + bias_ref[...]).astype(BF16)
        gates = z.astype(F32)
        if t > 0:
            gates = gates + matmul(h, w_rec_ref[...])
        i, f, g, o, c_new, tc = gated(gates, c)
        h = (o * tc).astype(BF16)
        hidden_ref[t] = h
        saved_ref[t, 0] = f
        saved_ref[t, 1] = o * (1.0 - tc * tc)
        saved_ref[t, 2] = g * i * (1.0 - i)
        saved_ref[t, 3] = c * f * (1.0 - f)
        saved_ref[t, 4] = i * (1.0 - g * g)
        saved_ref[t, 5] = tc * o * (1.0 - o)
        c = c_new
    copies = fetch(((hidden_ref.at[snap], hidden_hbm),), sems)
    dh = jnp.zeros((NODE, H), F32)
    dc = jnp.zeros((NODE, H), F32)
    for t in range(SNAPS - 1, -1, -1):
        at = (t & 1) * 4 + (t & 2) + (t >> 2)
        dh = dh + cot_ref[at].astype(F32)
        dc = dc + dh * saved_ref[t, 1]
        grad = jnp.concatenate(
            [dc * saved_ref[t, 2], dc * saved_ref[t, 3], dc * saved_ref[t, 4], dh * saved_ref[t, 5]],
            1,
        ).astype(BF16)
        grads_ref[t] = grad
        if t > 0:
            dh = matmul(grad, turned_ref[...])
            dc = dc * saved_ref[t, 0]
    copies += fetch(((grads_ref.at[snap], grads_hbm),), sems.at[pl.ds(1, 1)])
    for copy in copies:
        copy.wait()


def call(kernel, out, *args, scratch=(), limit=16, **more):
    return pl.pallas_call(
        kernel,
        out_shape=out,
        scratch_shapes=list(scratch),
        compiler_params=pltpu.CompilerParams(vmem_limit_bytes=limit * 1024 * 1024),
        **more,
    )(*args)


def shaped(shape, dtype=BF16):
    return jax.ShapeDtypeStruct(shape, dtype)


def exchange(array, axes):
    return lax.all_to_all(array, axes, 0, 0, tiled=True)


def shards(
    features, nbr_owner, nbr_row, counts, weight_one, weight_two, w_in, w_rec, gate_bias, cotangent
):
    chips = ("z", "x")
    hbm = pl.BlockSpec(memory_space=pltpu.HBM)
    vmem = pl.BlockSpec(memory_space=pltpu.VMEM)
    x = features[0]
    owner = nbr_owner.reshape(KNB, LANES)
    wanted, rank = call(
        plan_kernel,
        (shaped((CHIPS, LANES), F32), shaped((KNB, LANES), F32)),
        owner,
        nbr_row.reshape(KNB, LANES),
        in_specs=[hbm] * 2,
        scratch=(
            pltpu.VMEM((KNB, LANES), jnp.int32),
            pltpu.VMEM((KNB, LANES), jnp.int32),
            pltpu.SemaphoreType.DMA((2,)),
        ),
        limit=60,
    )
    asked = exchange(wanted, chips)
    pair = lax.all_gather(x, "core", tiled=True)
    asked, pair = lax.optimization_barrier((asked, pair))
    staged = (pltpu.VMEM((SLOTS, H), BF16), pltpu.SemaphoreType.DMA((BLOCKS,)))
    pick, outgoing = call(
        pick_kernel,
        (shaped((SLOTS, H)), shaped((SLOTS, H))),
        asked,
        pair,
        out_specs=[vmem, hbm],
        scratch=staged,
    )
    snap = lax.axis_index(TM).reshape(1).astype(jnp.int32)
    outgoing, cot, rank, snap = lax.optimization_barrier((outgoing, cotangent, rank, snap))
    arrived = exchange(outgoing.reshape(CHIPS, CAP, H), chips).reshape(SLOTS, H)
    cot = lax.all_gather(cot, "t2", tiled=True)
    cot = lax.all_gather(cot, "t1", tiled=True)
    comb = call(comb_kernel, shaped((NODE, SLOTS)), rank, owner, counts)
    comb, cot = lax.optimization_barrier((comb, cot))
    x = call(first_kernel, shaped((NODE, H)), comb, arrived, x, counts, weight_one)
    pair = lax.all_gather(x, "core", tiled=True)
    outgoing = call(
        again_kernel, shaped((SLOTS, H)), pick, pair, out_specs=hbm, scratch=staged
    )
    outgoing, cot = lax.optimization_barrier((outgoing, cot))
    arrived = exchange(outgoing.reshape(CHIPS, CAP, H), chips).reshape(SLOTS, H)
    cot = lax.all_gather(cot, "t0", tiled=True)
    comb, cot = lax.optimization_barrier((comb, cot))
    copies = call(
        second_kernel, shaped((SNAPS, NODE, H)), comb, arrived, x, counts, weight_two
    )
    xs = exchange(copies, TM)
    hidden, grads = call(
        chain_kernel,
        (shaped((NODE, H)), shaped((NODE, 4 * H))),
        xs,
        cot,
        w_in,
        w_rec,
        gate_bias.reshape(1, 4 * H),
        snap,
        in_specs=[vmem] * 5 + [pl.BlockSpec(memory_space=pltpu.SMEM)],
        out_specs=[hbm] * 2,
        scratch=(
            pltpu.VMEM((SNAPS, 6, NODE, H), F32),
            pltpu.VMEM((4 * H, H), BF16),
            pltpu.VMEM((SNAPS, NODE, H), BF16),
            pltpu.VMEM((SNAPS, NODE, 4 * H), BF16),
            pltpu.SemaphoreType.DMA((2,)),
        ),
    )
    return hidden[None], grads[None]
def solution(mesh):
    mesh = Mesh(mesh.devices.reshape(2, 2, 2, 8, 4, 2), TM + ("z", "x", "core"))
    acct = ("z", "x", "core")
    return jax.shard_map(
        shards,
        mesh=mesh,
        in_specs=(
            P(TM, acct, None),
            P(TM, acct, None),
            P(TM, acct),
            P(TM, acct),
            P(),
            P(),
            P(),
            P(),
            P(),
            P(TM, acct, None),
        ),
        out_specs=(P(TM, acct, None), P(TM, acct, None)),
        check_vma=False,
    )
```

```python
import jax
import jax.numpy as jnp
from jax import lax
from jax.experimental import pallas as pl
from jax.experimental.pallas import tpu as pltpu
from jax.sharding import Mesh
from jax.sharding import PartitionSpec as P

H = 256
KNB = 8
NODE = 128
SNAPS = 8
CHIPS = 32
CAP = 40
SLOTS = CHIPS * CAP
BLOCKS = 8
TM = ("t2", "t1", "t0")
LANES = 128
BF16 = jnp.bfloat16
F32 = jnp.float32
NT = ((1,), (1,))


def iota(shape, dim):
    return lax.broadcasted_iota(jnp.int32, shape, dim)


def matmul(a, b, dims=((1,), (0,))):
    return lax.dot_general(a, b, (dims, ((), ())), preferred_element_type=F32)


def fetch(pairs, sems):
    copies = [pltpu.make_async_copy(a, b, sems.at[i]) for i, (a, b) in enumerate(pairs)]
    for copy in copies:
        copy.start()
    return copies


def plan_kernel(owner_hbm, row_hbm, wanted_ref, rank_ref, owner_ref, row_ref, sems):
    for copy in fetch(((owner_hbm, owner_ref), (row_hbm, row_ref)), sems):
        copy.wait()
    owner = owner_ref[...]
    value = ((owner % 2) * NODE + row_ref[...]).astype(F32)
    chip = owner // 2
    upper = jnp.where(iota((LANES, LANES), 0) < iota((LANES, LANES), 1), 1.0, 0.0).astype(BF16)
    named = [
        jnp.where(iota((CHIPS, LANES), 0) == chip[i : i + 1, :], 1.0, 0.0) for i in range(KNB)
    ]
    before = matmul(jnp.concatenate(named, 0).astype(BF16), upper)
    base = jnp.zeros((CHIPS, 1), F32)
    wanted = jnp.zeros((CHIPS, LANES), F32)
    for i in range(KNB):
        earlier = before[i * CHIPS : (i + 1) * CHIPS] + base
        base = base + jnp.sum(named[i], 1, keepdims=True)
        rank = jnp.sum(named[i] * earlier, 0, keepdims=True)
        rank_ref[i : i + 1, :] = rank
        ranks = jnp.where(iota((LANES, LANES), 0).astype(F32) == rank, 1.0, 0.0).astype(BF16)
        wanted = wanted + matmul((named[i] * value[i : i + 1, :]).astype(BF16), ranks, NT)
    wanted_ref[...] = wanted


def column(row):
    eye = iota((NODE, NODE), 0) == iota((NODE, NODE), 1)
    return jnp.sum(jnp.where(eye, row, 0.0), 1, keepdims=True)


def comb_kernel(rank_ref, owner_ref, cnt_ref, comb_ref):
    count = column(cnt_ref[...].astype(F32))
    lane = iota((1, LANES), 1)
    sub = iota((2 * KNB, LANES), 0)
    chip = (owner_ref[...] // 2).astype(F32)
    place = jnp.zeros((NODE, 2 * KNB), F32)
    for i in range(KNB):
        group = jnp.where(iota((NODE, LANES), 0) == i * (LANES // KNB) + lane // KNB, 1.0, 0.0)
        coded = jnp.where(sub < KNB, chip[i : i + 1, :], rank_ref[i : i + 1, :])
        coded = jnp.where(sub % KNB == lane % KNB, coded, 0.0)
        place = place + matmul(group.astype(BF16), coded.astype(BF16), NT)
    place = place[:, :KNB] * CAP + place[:, KNB:]
    place = jnp.where(iota((NODE, KNB), 1).astype(F32) < count, place, -1.0)
    spot = iota((NODE, SLOTS), 1).astype(F32)
    comb = jnp.zeros((NODE, SLOTS), F32)
    for k in range(KNB):
        comb = comb + jnp.where(spot == place[:, k : k + 1], 1.0, 0.0)
    comb_ref[...] = comb.astype(BF16)


def pick_kernel(asked_ref, x_ref, pick_ref, out_hbm, out_ref, sems):
    eye = jnp.where(iota((LANES, LANES), 0) == iota((LANES, LANES), 1), 1.0, 0.0).astype(BF16)
    turned = matmul(eye, asked_ref[...].astype(BF16), NT)
    col = iota((CAP, H), 1).astype(F32)
    x = x_ref[...]
    copies = []
    for block in range(BLOCKS):
        rows = slice(block * SLOTS // BLOCKS, (block + 1) * SLOTS // BLOCKS)
        chips = range(block * CHIPS // BLOCKS, (block + 1) * CHIPS // BLOCKS)
        named = [jnp.where(turned[:CAP, d : d + 1] == col, 1.0, 0.0) for d in chips]
        pick = jnp.concatenate(named, 0).astype(BF16)
        pick_ref[rows, :] = pick
        out_ref[rows, :] = matmul(pick, x).astype(BF16)
        copies += fetch(((out_ref.at[rows, :], out_hbm.at[rows, :]),), sems.at[pl.ds(block, 1)])
    for copy in copies:
        copy.wait()


def again_kernel(pick_ref, x_ref, out_hbm, out_ref, sems):
    x = x_ref[...]
    copies = []
    for block in range(BLOCKS):
        rows = slice(block * SLOTS // BLOCKS, (block + 1) * SLOTS // BLOCKS)
        out_ref[rows, :] = matmul(pick_ref[rows, :], x).astype(BF16)
        copies += fetch(((out_ref.at[rows, :], out_hbm.at[rows, :]),), sems.at[pl.ds(block, 1)])
    for copy in copies:
        copy.wait()


def convolved(comb_ref, arrived_ref, x_ref, cnt_ref, weight_ref):
    count = column(cnt_ref[...].astype(F32))
    summed = x_ref[...].astype(F32) + matmul(comb_ref[...], arrived_ref[...])
    agg = (summed * (1.0 / (count + 1.0))).astype(BF16)
    return jnp.maximum(matmul(agg, weight_ref[...]), 0.0).astype(BF16)


def first_kernel(*refs):
    refs[-1][...] = convolved(*refs[:-1])


def second_kernel(*refs):
    x = convolved(*refs[:-1])
    for t in range(SNAPS):
        refs[-1][t] = x


def gated(gates, c):
    i = jax.nn.sigmoid(gates[:, :H])
    f = jax.nn.sigmoid(gates[:, H : 2 * H])
    g = jnp.tanh(gates[:, 2 * H : 3 * H])
    o = jax.nn.sigmoid(gates[:, 3 * H :])
    c_new = f * c + i * g
    return i, f, g, o, c_new, jnp.tanh(c_new)


def chain_kernel(
    x_ref,
    cot_ref,
    w_in_ref,
    w_rec_ref,
    bias_ref,
    snap_ref,
    hidden_hbm,
    grads_hbm,
    saved_ref,
    turned_ref,
    hidden_ref,
    grads_ref,
    sems,
):
    snap = snap_ref[0]
    turned_ref[...] = w_rec_ref[...].T
    h = None
    c = jnp.zeros((NODE, H), F32)
    for t in range(SNAPS):
        z = (matmul(x_ref[t], w_in_ref[...]) + bias_ref[...]).astype(BF16)
        gates = z.astype(F32)
        if t > 0:
            gates = gates + matmul(h, w_rec_ref[...])
        i, f, g, o, c_new, tc = gated(gates, c)
        h = (o * tc).astype(BF16)
        hidden_ref[t] = h
        saved_ref[t, 0] = f
        saved_ref[t, 1] = o * (1.0 - tc * tc)
        saved_ref[t, 2] = g * i * (1.0 - i)
        saved_ref[t, 3] = c * f * (1.0 - f)
        saved_ref[t, 4] = i * (1.0 - g * g)
        saved_ref[t, 5] = tc * o * (1.0 - o)
        c = c_new
    copies = fetch(((hidden_ref.at[snap], hidden_hbm),), sems)
    dh = jnp.zeros((NODE, H), F32)
    dc = jnp.zeros((NODE, H), F32)
    for t in range(SNAPS - 1, -1, -1):
        at = (t & 1) * 4 + (t & 2) + (t >> 2)
        dh = dh + cot_ref[at].astype(F32)
        dc = dc + dh * saved_ref[t, 1]
        grad = jnp.concatenate(
            [dc * saved_ref[t, 2], dc * saved_ref[t, 3], dc * saved_ref[t, 4], dh * saved_ref[t, 5]],
            1,
        ).astype(BF16)
        grads_ref[t] = grad
        if t > 0:
            dh = matmul(grad, turned_ref[...])
            dc = dc * saved_ref[t, 0]
    copies += fetch(((grads_ref.at[snap], grads_hbm),), sems.at[pl.ds(1, 1)])
    for copy in copies:
        copy.wait()


def call(kernel, out, *args, scratch=(), limit=16, **more):
    return pl.pallas_call(
        kernel,
        out_shape=out,
        scratch_shapes=list(scratch),
        compiler_params=pltpu.CompilerParams(vmem_limit_bytes=limit * 1024 * 1024),
        **more,
    )(*args)


def shaped(shape, dtype=BF16):
    return jax.ShapeDtypeStruct(shape, dtype)


def exchange(array, axes):
    return lax.all_to_all(array, axes, 0, 0, tiled=True)


def shards(
    features, nbr_owner, nbr_row, counts, weight_one, weight_two, w_in, w_rec, gate_bias, cotangent
):
    chips = ("z", "x")
    hbm = pl.BlockSpec(memory_space=pltpu.HBM)
    vmem = pl.BlockSpec(memory_space=pltpu.VMEM)
    x = features[0]
    owner = nbr_owner.reshape(KNB, LANES)
    wanted, rank = call(
        plan_kernel,
        (shaped((CHIPS, LANES), F32), shaped((KNB, LANES), F32)),
        owner,
        nbr_row.reshape(KNB, LANES),
        in_specs=[hbm] * 2,
        scratch=(
            pltpu.VMEM((KNB, LANES), jnp.int32),
            pltpu.VMEM((KNB, LANES), jnp.int32),
            pltpu.SemaphoreType.DMA((2,)),
        ),
        limit=60,
    )
    asked = exchange(wanted, chips)
    pair = lax.all_gather(x, "core", tiled=True)
    asked, pair = lax.optimization_barrier((asked, pair))
    staged = (pltpu.VMEM((SLOTS, H), BF16), pltpu.SemaphoreType.DMA((BLOCKS,)))
    pick, outgoing = call(
        pick_kernel,
        (shaped((SLOTS, H)), shaped((SLOTS, H))),
        asked,
        pair,
        out_specs=[vmem, hbm],
        scratch=staged,
    )
    snap = lax.axis_index(TM).reshape(1).astype(jnp.int32)
    outgoing, cot, rank, snap = lax.optimization_barrier((outgoing, cotangent, rank, snap))
    arrived = exchange(outgoing.reshape(CHIPS, CAP, H), chips).reshape(SLOTS, H)
    cot = lax.all_gather(cot, "t2", tiled=True)
    comb = call(comb_kernel, shaped((NODE, SLOTS)), rank, owner, counts)
    comb, cot = lax.optimization_barrier((comb, cot))
    x = call(first_kernel, shaped((NODE, H)), comb, arrived, x, counts, weight_one)
    pair = lax.all_gather(x, "core", tiled=True)
    outgoing = call(
        again_kernel, shaped((SLOTS, H)), pick, pair, out_specs=hbm, scratch=staged
    )
    outgoing, cot = lax.optimization_barrier((outgoing, cot))
    arrived = exchange(outgoing.reshape(CHIPS, CAP, H), chips).reshape(SLOTS, H)
    cot = lax.all_gather(cot, "t1", tiled=True)
    cot = lax.all_gather(cot, "t0", tiled=True)
    comb, cot = lax.optimization_barrier((comb, cot))
    copies = call(
        second_kernel, shaped((SNAPS, NODE, H)), comb, arrived, x, counts, weight_two
    )
    xs = exchange(copies, TM)
    hidden, grads = call(
        chain_kernel,
        (shaped((NODE, H)), shaped((NODE, 4 * H))),
        xs,
        cot,
        w_in,
        w_rec,
        gate_bias.reshape(1, 4 * H),
        snap,
        in_specs=[vmem] * 5 + [pl.BlockSpec(memory_space=pltpu.SMEM)],
        out_specs=[hbm] * 2,
        scratch=(
            pltpu.VMEM((SNAPS, 6, NODE, H), F32),
            pltpu.VMEM((4 * H, H), BF16),
            pltpu.VMEM((SNAPS, NODE, H), BF16),
            pltpu.VMEM((SNAPS, NODE, 4 * H), BF16),
            pltpu.SemaphoreType.DMA((2,)),
        ),
    )
    return hidden[None], grads[None]
def solution(mesh):
    mesh = Mesh(mesh.devices.reshape(2, 2, 2, 8, 4, 2), TM + ("z", "x", "core"))
    acct = ("z", "x", "core")
    return jax.shard_map(
        shards,
        mesh=mesh,
        in_specs=(
            P(TM, acct, None),
            P(TM, acct, None),
            P(TM, acct),
            P(TM, acct),
            P(),
            P(),
            P(),
            P(),
            P(),
            P(TM, acct, None),
        ),
        out_specs=(P(TM, acct, None), P(TM, acct, None)),
        check_vma=False,
    )
```

```python
import jax
import jax.numpy as jnp
from jax import lax
from jax.experimental import pallas as pl
from jax.experimental.pallas import tpu as pltpu
from jax.sharding import Mesh
from jax.sharding import PartitionSpec as P

H = 256
KNB = 8
NODE = 128
SNAPS = 8
CHIPS = 32
CAP = 40
SLOTS = CHIPS * CAP
BLOCKS = 8
TM = ("t2", "t1", "t0")
LANES = 128
BF16 = jnp.bfloat16
F32 = jnp.float32
NT = ((1,), (1,))


def iota(shape, dim):
    return lax.broadcasted_iota(jnp.int32, shape, dim)


def matmul(a, b, dims=((1,), (0,))):
    return lax.dot_general(a, b, (dims, ((), ())), preferred_element_type=F32)


def fetch(pairs, sems):
    copies = [pltpu.make_async_copy(a, b, sems.at[i]) for i, (a, b) in enumerate(pairs)]
    for copy in copies:
        copy.start()
    return copies


def plan_kernel(owner_hbm, row_hbm, wanted_ref, rank_ref, owner_ref, row_ref, sems):
    for copy in fetch(((owner_hbm, owner_ref), (row_hbm, row_ref)), sems):
        copy.wait()
    owner = owner_ref[...]
    value = ((owner % 2) * NODE + row_ref[...]).astype(F32)
    chip = owner // 2
    upper = jnp.where(iota((LANES, LANES), 0) < iota((LANES, LANES), 1), 1.0, 0.0).astype(BF16)
    named = [
        jnp.where(iota((CHIPS, LANES), 0) == chip[i : i + 1, :], 1.0, 0.0) for i in range(KNB)
    ]
    before = matmul(jnp.concatenate(named, 0).astype(BF16), upper)
    base = jnp.zeros((CHIPS, 1), F32)
    wanted = jnp.zeros((CHIPS, LANES), F32)
    for i in range(KNB):
        earlier = before[i * CHIPS : (i + 1) * CHIPS] + base
        base = base + jnp.sum(named[i], 1, keepdims=True)
        rank = jnp.sum(named[i] * earlier, 0, keepdims=True)
        rank_ref[i : i + 1, :] = rank
        ranks = jnp.where(iota((LANES, LANES), 0).astype(F32) == rank, 1.0, 0.0).astype(BF16)
        wanted = wanted + matmul((named[i] * value[i : i + 1, :]).astype(BF16), ranks, NT)
    wanted_ref[...] = wanted


def column(row):
    eye = iota((NODE, NODE), 0) == iota((NODE, NODE), 1)
    return jnp.sum(jnp.where(eye, row, 0.0), 1, keepdims=True)


def comb_kernel(rank_ref, owner_ref, cnt_ref, comb_ref):
    count = column(cnt_ref[...].astype(F32))
    lane = iota((1, LANES), 1)
    sub = iota((2 * KNB, LANES), 0)
    chip = (owner_ref[...] // 2).astype(F32)
    place = jnp.zeros((NODE, 2 * KNB), F32)
    for i in range(KNB):
        group = jnp.where(iota((NODE, LANES), 0) == i * (LANES // KNB) + lane // KNB, 1.0, 0.0)
        coded = jnp.where(sub < KNB, chip[i : i + 1, :], rank_ref[i : i + 1, :])
        coded = jnp.where(sub % KNB == lane % KNB, coded, 0.0)
        place = place + matmul(group.astype(BF16), coded.astype(BF16), NT)
    place = place[:, :KNB] * CAP + place[:, KNB:]
    place = jnp.where(iota((NODE, KNB), 1).astype(F32) < count, place, -1.0)
    spot = iota((NODE, SLOTS), 1).astype(F32)
    comb = jnp.zeros((NODE, SLOTS), F32)
    for k in range(KNB):
        comb = comb + jnp.where(spot == place[:, k : k + 1], 1.0, 0.0)
    comb_ref[...] = comb.astype(BF16)


def pick_kernel(asked_ref, x_ref, pick_ref, out_hbm, out_ref, sems):
    eye = jnp.where(iota((LANES, LANES), 0) == iota((LANES, LANES), 1), 1.0, 0.0).astype(BF16)
    turned = matmul(eye, asked_ref[...].astype(BF16), NT)
    col = iota((CAP, H), 1).astype(F32)
    x = x_ref[...]
    copies = []
    for block in range(BLOCKS):
        rows = slice(block * SLOTS // BLOCKS, (block + 1) * SLOTS // BLOCKS)
        chips = range(block * CHIPS // BLOCKS, (block + 1) * CHIPS // BLOCKS)
        named = [jnp.where(turned[:CAP, d : d + 1] == col, 1.0, 0.0) for d in chips]
        pick = jnp.concatenate(named, 0).astype(BF16)
        pick_ref[rows, :] = pick
        out_ref[rows, :] = matmul(pick, x).astype(BF16)
        copies += fetch(((out_ref.at[rows, :], out_hbm.at[rows, :]),), sems.at[pl.ds(block, 1)])
    for copy in copies:
        copy.wait()


def again_kernel(pick_ref, x_ref, out_hbm, out_ref, sems):
    x = x_ref[...]
    copies = []
    for block in range(BLOCKS):
        rows = slice(block * SLOTS // BLOCKS, (block + 1) * SLOTS // BLOCKS)
        out_ref[rows, :] = matmul(pick_ref[rows, :], x).astype(BF16)
        copies += fetch(((out_ref.at[rows, :], out_hbm.at[rows, :]),), sems.at[pl.ds(block, 1)])
    for copy in copies:
        copy.wait()


def convolved(comb_ref, arrived_ref, x_ref, cnt_ref, weight_ref):
    count = column(cnt_ref[...].astype(F32))
    summed = x_ref[...].astype(F32) + matmul(comb_ref[...], arrived_ref[...])
    agg = (summed * (1.0 / (count + 1.0))).astype(BF16)
    return jnp.maximum(matmul(agg, weight_ref[...]), 0.0).astype(BF16)


def first_kernel(*refs):
    refs[-1][...] = convolved(*refs[:-1])


def second_kernel(*refs):
    x = convolved(*refs[:-1])
    for t in range(SNAPS):
        refs[-1][t] = x


def gated(gates, c):
    i = jax.nn.sigmoid(gates[:, :H])
    f = jax.nn.sigmoid(gates[:, H : 2 * H])
    g = jnp.tanh(gates[:, 2 * H : 3 * H])
    o = jax.nn.sigmoid(gates[:, 3 * H :])
    c_new = f * c + i * g
    return i, f, g, o, c_new, jnp.tanh(c_new)


def turned_bits(t):
    return (t & 1) * 4 + (t & 2) + (t >> 2)


def chain_kernel(
    x_ref,
    cot_ref,
    w_in_ref,
    w_rec_ref,
    bias_ref,
    snap_ref,
    hidden_hbm,
    grads_hbm,
    saved_ref,
    turned_ref,
    hidden_ref,
    grads_ref,
    sems,
):
    snap = snap_ref[0]
    turned_ref[...] = w_rec_ref[...].T
    h = None
    c = jnp.zeros((NODE, H), F32)
    for t in range(SNAPS):
        z = (matmul(x_ref[turned_bits(t)], w_in_ref[...]) + bias_ref[...]).astype(BF16)
        gates = z.astype(F32)
        if t > 0:
            gates = gates + matmul(h, w_rec_ref[...])
        i, f, g, o, c_new, tc = gated(gates, c)
        h = (o * tc).astype(BF16)
        hidden_ref[t] = h
        saved_ref[t, 0] = f
        saved_ref[t, 1] = o * (1.0 - tc * tc)
        saved_ref[t, 2] = g * i * (1.0 - i)
        saved_ref[t, 3] = c * f * (1.0 - f)
        saved_ref[t, 4] = i * (1.0 - g * g)
        saved_ref[t, 5] = tc * o * (1.0 - o)
        c = c_new
    copies = fetch(((hidden_ref.at[snap], hidden_hbm),), sems)
    dh = jnp.zeros((NODE, H), F32)
    dc = jnp.zeros((NODE, H), F32)
    for t in range(SNAPS - 1, -1, -1):
        dh = dh + cot_ref[turned_bits(t)].astype(F32)
        dc = dc + dh * saved_ref[t, 1]
        grad = jnp.concatenate(
            [dc * saved_ref[t, 2], dc * saved_ref[t, 3], dc * saved_ref[t, 4], dh * saved_ref[t, 5]],
            1,
        ).astype(BF16)
        grads_ref[t] = grad
        if t > 0:
            dh = matmul(grad, turned_ref[...])
            dc = dc * saved_ref[t, 0]
    copies += fetch(((grads_ref.at[snap], grads_hbm),), sems.at[pl.ds(1, 1)])
    for copy in copies:
        copy.wait()


def call(kernel, out, *args, scratch=(), limit=16, **more):
    return pl.pallas_call(
        kernel,
        out_shape=out,
        scratch_shapes=list(scratch),
        compiler_params=pltpu.CompilerParams(vmem_limit_bytes=limit * 1024 * 1024),
        **more,
    )(*args)


def shaped(shape, dtype=BF16):
    return jax.ShapeDtypeStruct(shape, dtype)


def exchange(array, axes):
    return lax.all_to_all(array, axes, 0, 0, tiled=True)


def shards(
    features, nbr_owner, nbr_row, counts, weight_one, weight_two, w_in, w_rec, gate_bias, cotangent
):
    chips = ("z", "x")
    hbm = pl.BlockSpec(memory_space=pltpu.HBM)
    vmem = pl.BlockSpec(memory_space=pltpu.VMEM)
    x = features[0]
    owner = nbr_owner.reshape(KNB, LANES)
    wanted, rank = call(
        plan_kernel,
        (shaped((CHIPS, LANES), F32), shaped((KNB, LANES), F32)),
        owner,
        nbr_row.reshape(KNB, LANES),
        in_specs=[hbm] * 2,
        scratch=(
            pltpu.VMEM((KNB, LANES), jnp.int32),
            pltpu.VMEM((KNB, LANES), jnp.int32),
            pltpu.SemaphoreType.DMA((2,)),
        ),
        limit=60,
    )
    asked = exchange(wanted, chips)
    pair = lax.all_gather(x, "core", tiled=True)
    asked, pair = lax.optimization_barrier((asked, pair))
    staged = (pltpu.VMEM((SLOTS, H), BF16), pltpu.SemaphoreType.DMA((BLOCKS,)))
    pick, outgoing = call(
        pick_kernel,
        (shaped((SLOTS, H)), shaped((SLOTS, H))),
        asked,
        pair,
        out_specs=[vmem, hbm],
        scratch=staged,
    )
    snap = lax.axis_index(TM).reshape(1).astype(jnp.int32)
    outgoing, cot, rank, snap = lax.optimization_barrier((outgoing, cotangent, rank, snap))
    arrived = exchange(outgoing.reshape(CHIPS, CAP, H), chips).reshape(SLOTS, H)
    cot = lax.all_gather(cot, "t2", tiled=True)
    comb = call(comb_kernel, shaped((NODE, SLOTS)), rank, owner, counts)
    comb, cot = lax.optimization_barrier((comb, cot))
    x = call(first_kernel, shaped((NODE, H)), comb, arrived, x, counts, weight_one)
    pair = lax.all_gather(x, "core", tiled=True)
    outgoing = call(
        again_kernel, shaped((SLOTS, H)), pick, pair, out_specs=hbm, scratch=staged
    )
    outgoing, cot = lax.optimization_barrier((outgoing, cot))
    arrived = exchange(outgoing.reshape(CHIPS, CAP, H), chips).reshape(SLOTS, H)
    cot = lax.all_gather(cot, "t1", tiled=True)
    cot = lax.all_gather(cot, "t0", tiled=True)
    comb, cot = lax.optimization_barrier((comb, cot))
    copies = call(
        second_kernel, shaped((SNAPS, NODE, H)), comb, arrived, x, counts, weight_two
    )
    xs = exchange(copies, TM[::-1])
    hidden, grads = call(
        chain_kernel,
        (shaped((NODE, H)), shaped((NODE, 4 * H))),
        xs,
        cot,
        w_in,
        w_rec,
        gate_bias.reshape(1, 4 * H),
        snap,
        in_specs=[vmem] * 5 + [pl.BlockSpec(memory_space=pltpu.SMEM)],
        out_specs=[hbm] * 2,
        scratch=(
            pltpu.VMEM((SNAPS, 6, NODE, H), F32),
            pltpu.VMEM((4 * H, H), BF16),
            pltpu.VMEM((SNAPS, NODE, H), BF16),
            pltpu.VMEM((SNAPS, NODE, 4 * H), BF16),
            pltpu.SemaphoreType.DMA((2,)),
        ),
    )
    return hidden[None], grads[None]
def solution(mesh):
    mesh = Mesh(mesh.devices.reshape(2, 2, 2, 8, 4, 2), TM + ("z", "x", "core"))
    acct = ("z", "x", "core")
    return jax.shard_map(
        shards,
        mesh=mesh,
        in_specs=(
            P(TM, acct, None),
            P(TM, acct, None),
            P(TM, acct),
            P(TM, acct),
            P(),
            P(),
            P(),
            P(),
            P(),
            P(TM, acct, None),
        ),
        out_specs=(P(TM, acct, None), P(TM, acct, None)),
        check_vma=False,
    )
```

```python
import jax
import jax.numpy as jnp
from jax import lax
from jax.experimental import pallas as pl
from jax.experimental.pallas import tpu as pltpu
from jax.sharding import Mesh
from jax.sharding import PartitionSpec as P

H = 256
KNB = 8
NODE = 128
SNAPS = 8
CHIPS = 32
CAP = 40
SLOTS = CHIPS * CAP
BLOCKS = 8
TM = ("t2", "t1", "t0")
LANES = 128
BF16 = jnp.bfloat16
F32 = jnp.float32
NT = ((1,), (1,))


def iota(shape, dim):
    return lax.broadcasted_iota(jnp.int32, shape, dim)


def matmul(a, b, dims=((1,), (0,))):
    return lax.dot_general(a, b, (dims, ((), ())), preferred_element_type=F32)


def fetch(pairs, sems):
    copies = [pltpu.make_async_copy(a, b, sems.at[i]) for i, (a, b) in enumerate(pairs)]
    for copy in copies:
        copy.start()
    return copies


def chip_of(owner):
    return owner // 2 % 4 * 8 + owner // 8


def plan_kernel(owner_hbm, row_hbm, wanted_ref, rank_ref, owner_ref, row_ref, sems):
    for copy in fetch(((owner_hbm, owner_ref), (row_hbm, row_ref)), sems):
        copy.wait()
    owner = owner_ref[...]
    value = ((owner % 2) * NODE + row_ref[...]).astype(F32)
    chip = chip_of(owner)
    upper = jnp.where(iota((LANES, LANES), 0) < iota((LANES, LANES), 1), 1.0, 0.0).astype(BF16)
    named = [
        jnp.where(iota((CHIPS, LANES), 0) == chip[i : i + 1, :], 1.0, 0.0) for i in range(KNB)
    ]
    before = matmul(jnp.concatenate(named, 0).astype(BF16), upper)
    base = jnp.zeros((CHIPS, 1), F32)
    wanted = jnp.zeros((CHIPS, LANES), F32)
    for i in range(KNB):
        earlier = before[i * CHIPS : (i + 1) * CHIPS] + base
        base = base + jnp.sum(named[i], 1, keepdims=True)
        rank = jnp.sum(named[i] * earlier, 0, keepdims=True)
        rank_ref[i : i + 1, :] = rank
        ranks = jnp.where(iota((LANES, LANES), 0).astype(F32) == rank, 1.0, 0.0).astype(BF16)
        wanted = wanted + matmul((named[i] * value[i : i + 1, :]).astype(BF16), ranks, NT)
    wanted_ref[...] = wanted


def column(row):
    eye = iota((NODE, NODE), 0) == iota((NODE, NODE), 1)
    return jnp.sum(jnp.where(eye, row, 0.0), 1, keepdims=True)


def comb_kernel(rank_ref, owner_ref, cnt_ref, comb_ref):
    count = column(cnt_ref[...].astype(F32))
    lane = iota((1, LANES), 1)
    sub = iota((2 * KNB, LANES), 0)
    chip = chip_of(owner_ref[...]).astype(F32)
    place = jnp.zeros((NODE, 2 * KNB), F32)
    for i in range(KNB):
        group = jnp.where(iota((NODE, LANES), 0) == i * (LANES // KNB) + lane // KNB, 1.0, 0.0)
        coded = jnp.where(sub < KNB, chip[i : i + 1, :], rank_ref[i : i + 1, :])
        coded = jnp.where(sub % KNB == lane % KNB, coded, 0.0)
        place = place + matmul(group.astype(BF16), coded.astype(BF16), NT)
    place = place[:, :KNB] * CAP + place[:, KNB:]
    place = jnp.where(iota((NODE, KNB), 1).astype(F32) < count, place, -1.0)
    spot = iota((NODE, SLOTS), 1).astype(F32)
    comb = jnp.zeros((NODE, SLOTS), F32)
    for k in range(KNB):
        comb = comb + jnp.where(spot == place[:, k : k + 1], 1.0, 0.0)
    comb_ref[...] = comb.astype(BF16)


def pick_kernel(asked_ref, x_ref, pick_ref, out_hbm, out_ref, sems):
    eye = jnp.where(iota((LANES, LANES), 0) == iota((LANES, LANES), 1), 1.0, 0.0).astype(BF16)
    turned = matmul(eye, asked_ref[...].astype(BF16), NT)
    col = iota((CAP, H), 1).astype(F32)
    x = x_ref[...]
    copies = []
    for block in range(BLOCKS):
        rows = slice(block * SLOTS // BLOCKS, (block + 1) * SLOTS // BLOCKS)
        chips = range(block * CHIPS // BLOCKS, (block + 1) * CHIPS // BLOCKS)
        named = [jnp.where(turned[:CAP, d : d + 1] == col, 1.0, 0.0) for d in chips]
        pick = jnp.concatenate(named, 0).astype(BF16)
        pick_ref[rows, :] = pick
        out_ref[rows, :] = matmul(pick, x).astype(BF16)
        copies += fetch(((out_ref.at[rows, :], out_hbm.at[rows, :]),), sems.at[pl.ds(block, 1)])
    for copy in copies:
        copy.wait()


def again_kernel(pick_ref, x_ref, out_hbm, out_ref, sems):
    x = x_ref[...]
    copies = []
    for block in range(BLOCKS):
        rows = slice(block * SLOTS // BLOCKS, (block + 1) * SLOTS // BLOCKS)
        out_ref[rows, :] = matmul(pick_ref[rows, :], x).astype(BF16)
        copies += fetch(((out_ref.at[rows, :], out_hbm.at[rows, :]),), sems.at[pl.ds(block, 1)])
    for copy in copies:
        copy.wait()


def convolved(comb_ref, arrived_ref, x_ref, cnt_ref, weight_ref):
    count = column(cnt_ref[...].astype(F32))
    summed = x_ref[...].astype(F32) + matmul(comb_ref[...], arrived_ref[...])
    agg = (summed * (1.0 / (count + 1.0))).astype(BF16)
    return jnp.maximum(matmul(agg, weight_ref[...]), 0.0).astype(BF16)


def first_kernel(*refs):
    refs[-1][...] = convolved(*refs[:-1])


def second_kernel(*refs):
    x = convolved(*refs[:-1])
    for t in range(SNAPS):
        refs[-1][t] = x


def gated(gates, c):
    i = jax.nn.sigmoid(gates[:, :H])
    f = jax.nn.sigmoid(gates[:, H : 2 * H])
    g = jnp.tanh(gates[:, 2 * H : 3 * H])
    o = jax.nn.sigmoid(gates[:, 3 * H :])
    c_new = f * c + i * g
    return i, f, g, o, c_new, jnp.tanh(c_new)


def turned_bits(t):
    return (t & 1) * 4 + (t & 2) + (t >> 2)


def chain_kernel(
    x_ref,
    cot_ref,
    w_in_ref,
    w_rec_ref,
    bias_ref,
    snap_ref,
    hidden_hbm,
    grads_hbm,
    saved_ref,
    turned_ref,
    hidden_ref,
    grads_ref,
    sems,
):
    snap = snap_ref[0]
    turned_ref[...] = w_rec_ref[...].T
    h = None
    c = jnp.zeros((NODE, H), F32)
    for t in range(SNAPS):
        z = (matmul(x_ref[turned_bits(t)], w_in_ref[...]) + bias_ref[...]).astype(BF16)
        gates = z.astype(F32)
        if t > 0:
            gates = gates + matmul(h, w_rec_ref[...])
        i, f, g, o, c_new, tc = gated(gates, c)
        h = (o * tc).astype(BF16)
        hidden_ref[t] = h
        saved_ref[t, 0] = f
        saved_ref[t, 1] = o * (1.0 - tc * tc)
        saved_ref[t, 2] = g * i * (1.0 - i)
        saved_ref[t, 3] = c * f * (1.0 - f)
        saved_ref[t, 4] = i * (1.0 - g * g)
        saved_ref[t, 5] = tc * o * (1.0 - o)
        c = c_new
    copies = fetch(((hidden_ref.at[snap], hidden_hbm),), sems)
    dh = jnp.zeros((NODE, H), F32)
    dc = jnp.zeros((NODE, H), F32)
    for t in range(SNAPS - 1, -1, -1):
        dh = dh + cot_ref[turned_bits(t)].astype(F32)
        dc = dc + dh * saved_ref[t, 1]
        grad = jnp.concatenate(
            [dc * saved_ref[t, 2], dc * saved_ref[t, 3], dc * saved_ref[t, 4], dh * saved_ref[t, 5]],
            1,
        ).astype(BF16)
        grads_ref[t] = grad
        if t > 0:
            dh = matmul(grad, turned_ref[...])
            dc = dc * saved_ref[t, 0]
    copies += fetch(((grads_ref.at[snap], grads_hbm),), sems.at[pl.ds(1, 1)])
    for copy in copies:
        copy.wait()


def call(kernel, out, *args, scratch=(), limit=16, **more):
    return pl.pallas_call(
        kernel,
        out_shape=out,
        scratch_shapes=list(scratch),
        compiler_params=pltpu.CompilerParams(vmem_limit_bytes=limit * 1024 * 1024),
        **more,
    )(*args)


def shaped(shape, dtype=BF16):
    return jax.ShapeDtypeStruct(shape, dtype)


def exchange(array, axes):
    return lax.all_to_all(array, axes, 0, 0, tiled=True)


def shards(
    features, nbr_owner, nbr_row, counts, weight_one, weight_two, w_in, w_rec, gate_bias, cotangent
):
    chips = ("x", "z")
    hbm = pl.BlockSpec(memory_space=pltpu.HBM)
    vmem = pl.BlockSpec(memory_space=pltpu.VMEM)
    x = features[0]
    owner = nbr_owner.reshape(KNB, LANES)
    wanted, rank = call(
        plan_kernel,
        (shaped((CHIPS, LANES), F32), shaped((KNB, LANES), F32)),
        owner,
        nbr_row.reshape(KNB, LANES),
        in_specs=[hbm] * 2,
        scratch=(
            pltpu.VMEM((KNB, LANES), jnp.int32),
            pltpu.VMEM((KNB, LANES), jnp.int32),
            pltpu.SemaphoreType.DMA((2,)),
        ),
        limit=60,
    )
    asked = exchange(wanted, chips)
    pair = lax.all_gather(x, "core", tiled=True)
    asked, pair = lax.optimization_barrier((asked, pair))
    staged = (pltpu.VMEM((SLOTS, H), BF16), pltpu.SemaphoreType.DMA((BLOCKS,)))
    pick, outgoing = call(
        pick_kernel,
        (shaped((SLOTS, H)), shaped((SLOTS, H))),
        asked,
        pair,
        out_specs=[vmem, hbm],
        scratch=staged,
    )
    snap = lax.axis_index(TM).reshape(1).astype(jnp.int32)
    outgoing, cot, rank, snap = lax.optimization_barrier((outgoing, cotangent, rank, snap))
    arrived = exchange(outgoing.reshape(CHIPS, CAP, H), chips).reshape(SLOTS, H)
    cot = lax.all_gather(cot, "t2", tiled=True)
    comb = call(comb_kernel, shaped((NODE, SLOTS)), rank, owner, counts)
    comb, cot = lax.optimization_barrier((comb, cot))
    x = call(first_kernel, shaped((NODE, H)), comb, arrived, x, counts, weight_one)
    pair = lax.all_gather(x, "core", tiled=True)
    outgoing = call(
        again_kernel, shaped((SLOTS, H)), pick, pair, out_specs=hbm, scratch=staged
    )
    outgoing, cot = lax.optimization_barrier((outgoing, cot))
    arrived = exchange(outgoing.reshape(CHIPS, CAP, H), chips).reshape(SLOTS, H)
    cot = lax.all_gather(cot, "t1", tiled=True)
    cot = lax.all_gather(cot, "t0", tiled=True)
    comb, cot = lax.optimization_barrier((comb, cot))
    copies = call(
        second_kernel, shaped((SNAPS, NODE, H)), comb, arrived, x, counts, weight_two
    )
    xs = exchange(copies, TM[::-1])
    hidden, grads = call(
        chain_kernel,
        (shaped((NODE, H)), shaped((NODE, 4 * H))),
        xs,
        cot,
        w_in,
        w_rec,
        gate_bias.reshape(1, 4 * H),
        snap,
        in_specs=[vmem] * 5 + [pl.BlockSpec(memory_space=pltpu.SMEM)],
        out_specs=[hbm] * 2,
        scratch=(
            pltpu.VMEM((SNAPS, 6, NODE, H), F32),
            pltpu.VMEM((4 * H, H), BF16),
            pltpu.VMEM((SNAPS, NODE, H), BF16),
            pltpu.VMEM((SNAPS, NODE, 4 * H), BF16),
            pltpu.SemaphoreType.DMA((2,)),
        ),
    )
    return hidden[None], grads[None]
def solution(mesh):
    mesh = Mesh(mesh.devices.reshape(2, 2, 2, 8, 4, 2), TM + ("z", "x", "core"))
    acct = ("z", "x", "core")
    return jax.shard_map(
        shards,
        mesh=mesh,
        in_specs=(
            P(TM, acct, None),
            P(TM, acct, None),
            P(TM, acct),
            P(TM, acct),
            P(),
            P(),
            P(),
            P(),
            P(),
            P(TM, acct, None),
        ),
        out_specs=(P(TM, acct, None), P(TM, acct, None)),
        check_vma=False,
    )
```

```python
import jax
import jax.numpy as jnp
from jax import lax
from jax.experimental import pallas as pl
from jax.experimental.pallas import tpu as pltpu
from jax.sharding import Mesh
from jax.sharding import PartitionSpec as P

H = 256
KNB = 8
NODE = 128
SNAPS = 8
CHIPS = 32
CAP = 40
SLOTS = CHIPS * CAP
BLOCKS = 8
TM = ("t2", "t1", "t0")
LANES = 128
RANKS = 64
BF16 = jnp.bfloat16
F32 = jnp.float32
NT = ((1,), (1,))


def iota(shape, dim):
    return lax.broadcasted_iota(jnp.int32, shape, dim)


def matmul(a, b, dims=((1,), (0,))):
    return lax.dot_general(a, b, (dims, ((), ())), preferred_element_type=F32)


def fetch(pairs, sems):
    copies = [pltpu.make_async_copy(a, b, sems.at[i]) for i, (a, b) in enumerate(pairs)]
    for copy in copies:
        copy.start()
    return copies


def chip_of(owner):
    return owner // 2 % 4 * 8 + owner // 8


def plan_kernel(owner_hbm, row_hbm, wanted_ref, rank_ref, owner_ref, row_ref, sems):
    for copy in fetch(((owner_hbm, owner_ref), (row_hbm, row_ref)), sems):
        copy.wait()
    owner = owner_ref[...]
    value = ((owner % 2) * NODE + row_ref[...]).astype(F32)
    chip = chip_of(owner)
    upper = jnp.where(iota((LANES, LANES), 0) < iota((LANES, LANES), 1), 1.0, 0.0).astype(BF16)
    named = [
        jnp.where(iota((CHIPS, LANES), 0) == chip[i : i + 1, :], 1.0, 0.0) for i in range(KNB)
    ]
    before = matmul(jnp.concatenate(named, 0).astype(BF16), upper)
    base = jnp.zeros((CHIPS, 1), F32)
    wanted = jnp.zeros((CHIPS, RANKS), F32)
    for i in range(KNB):
        earlier = before[i * CHIPS : (i + 1) * CHIPS] + base
        base = base + jnp.sum(named[i], 1, keepdims=True)
        rank = jnp.sum(named[i] * earlier, 0, keepdims=True)
        rank_ref[i : i + 1, :] = rank
        ranks = jnp.where(iota((RANKS, LANES), 0).astype(F32) == rank, 1.0, 0.0).astype(BF16)
        wanted = wanted + matmul((named[i] * value[i : i + 1, :]).astype(BF16), ranks, NT)
    wanted_ref[...] = wanted


def column(row):
    eye = iota((NODE, NODE), 0) == iota((NODE, NODE), 1)
    return jnp.sum(jnp.where(eye, row, 0.0), 1, keepdims=True)


def comb_kernel(rank_ref, owner_ref, cnt_ref, comb_ref):
    count = column(cnt_ref[...].astype(F32))
    lane = iota((1, LANES), 1)
    sub = iota((2 * KNB, LANES), 0)
    chip = chip_of(owner_ref[...]).astype(F32)
    place = jnp.zeros((NODE, 2 * KNB), F32)
    for i in range(KNB):
        group = jnp.where(iota((NODE, LANES), 0) == i * (LANES // KNB) + lane // KNB, 1.0, 0.0)
        coded = jnp.where(sub < KNB, chip[i : i + 1, :], rank_ref[i : i + 1, :])
        coded = jnp.where(sub % KNB == lane % KNB, coded, 0.0)
        place = place + matmul(group.astype(BF16), coded.astype(BF16), NT)
    place = place[:, :KNB] * CAP + place[:, KNB:]
    place = jnp.where(iota((NODE, KNB), 1).astype(F32) < count, place, -1.0)
    spot = iota((NODE, SLOTS), 1).astype(F32)
    comb = jnp.zeros((NODE, SLOTS), F32)
    for k in range(KNB):
        comb = comb + jnp.where(spot == place[:, k : k + 1], 1.0, 0.0)
    comb_ref[...] = comb.astype(BF16)


def pick_kernel(asked_ref, x_ref, pick_ref, out_hbm, out_ref, sems):
    eye = jnp.where(iota((RANKS, RANKS), 0) == iota((RANKS, RANKS), 1), 1.0, 0.0).astype(BF16)
    turned = matmul(eye, asked_ref[...].astype(BF16), NT)
    col = iota((CAP, H), 1).astype(F32)
    x = x_ref[...]
    copies = []
    for block in range(BLOCKS):
        rows = slice(block * SLOTS // BLOCKS, (block + 1) * SLOTS // BLOCKS)
        chips = range(block * CHIPS // BLOCKS, (block + 1) * CHIPS // BLOCKS)
        named = [jnp.where(turned[:CAP, d : d + 1] == col, 1.0, 0.0) for d in chips]
        pick = jnp.concatenate(named, 0).astype(BF16)
        pick_ref[rows, :] = pick
        out_ref[rows, :] = matmul(pick, x).astype(BF16)
        copies += fetch(((out_ref.at[rows, :], out_hbm.at[rows, :]),), sems.at[pl.ds(block, 1)])
    for copy in copies:
        copy.wait()


def again_kernel(pick_ref, x_ref, out_hbm, out_ref, sems):
    x = x_ref[...]
    copies = []
    for block in range(BLOCKS):
        rows = slice(block * SLOTS // BLOCKS, (block + 1) * SLOTS // BLOCKS)
        out_ref[rows, :] = matmul(pick_ref[rows, :], x).astype(BF16)
        copies += fetch(((out_ref.at[rows, :], out_hbm.at[rows, :]),), sems.at[pl.ds(block, 1)])
    for copy in copies:
        copy.wait()


def convolved(comb_ref, arrived_ref, x_ref, cnt_ref, weight_ref):
    count = column(cnt_ref[...].astype(F32))
    summed = x_ref[...].astype(F32) + matmul(comb_ref[...], arrived_ref[...])
    agg = (summed * (1.0 / (count + 1.0))).astype(BF16)
    return jnp.maximum(matmul(agg, weight_ref[...]), 0.0).astype(BF16)


def first_kernel(*refs):
    refs[-1][...] = convolved(*refs[:-1])


def second_kernel(*refs):
    x = convolved(*refs[:-1])
    for t in range(SNAPS):
        refs[-1][t] = x


def gated(gates, c):
    i = jax.nn.sigmoid(gates[:, :H])
    f = jax.nn.sigmoid(gates[:, H : 2 * H])
    g = jnp.tanh(gates[:, 2 * H : 3 * H])
    o = jax.nn.sigmoid(gates[:, 3 * H :])
    c_new = f * c + i * g
    return i, f, g, o, c_new, jnp.tanh(c_new)


def turned_bits(t):
    return (t & 1) * 4 + (t & 2) + (t >> 2)


def chain_kernel(
    x_ref,
    cot_ref,
    w_in_ref,
    w_rec_ref,
    bias_ref,
    snap_ref,
    hidden_hbm,
    grads_hbm,
    saved_ref,
    turned_ref,
    hidden_ref,
    grads_ref,
    sems,
):
    snap = snap_ref[0]
    turned_ref[...] = w_rec_ref[...].T
    h = None
    c = jnp.zeros((NODE, H), F32)
    for t in range(SNAPS):
        z = (matmul(x_ref[turned_bits(t)], w_in_ref[...]) + bias_ref[...]).astype(BF16)
        gates = z.astype(F32)
        if t > 0:
            gates = gates + matmul(h, w_rec_ref[...])
        i, f, g, o, c_new, tc = gated(gates, c)
        h = (o * tc).astype(BF16)
        hidden_ref[t] = h
        saved_ref[t, 0] = f
        saved_ref[t, 1] = o * (1.0 - tc * tc)
        saved_ref[t, 2] = g * i * (1.0 - i)
        saved_ref[t, 3] = c * f * (1.0 - f)
        saved_ref[t, 4] = i * (1.0 - g * g)
        saved_ref[t, 5] = tc * o * (1.0 - o)
        c = c_new
    copies = fetch(((hidden_ref.at[snap], hidden_hbm),), sems)
    dh = jnp.zeros((NODE, H), F32)
    dc = jnp.zeros((NODE, H), F32)
    for t in range(SNAPS - 1, -1, -1):
        dh = dh + cot_ref[turned_bits(t)].astype(F32)
        dc = dc + dh * saved_ref[t, 1]
        grad = jnp.concatenate(
            [dc * saved_ref[t, 2], dc * saved_ref[t, 3], dc * saved_ref[t, 4], dh * saved_ref[t, 5]],
            1,
        ).astype(BF16)
        grads_ref[t] = grad
        if t > 0:
            dh = matmul(grad, turned_ref[...])
            dc = dc * saved_ref[t, 0]
    copies += fetch(((grads_ref.at[snap], grads_hbm),), sems.at[pl.ds(1, 1)])
    for copy in copies:
        copy.wait()


def call(kernel, out, *args, scratch=(), limit=16, **more):
    return pl.pallas_call(
        kernel,
        out_shape=out,
        scratch_shapes=list(scratch),
        compiler_params=pltpu.CompilerParams(vmem_limit_bytes=limit * 1024 * 1024),
        **more,
    )(*args)


def shaped(shape, dtype=BF16):
    return jax.ShapeDtypeStruct(shape, dtype)


def exchange(array, axes):
    return lax.all_to_all(array, axes, 0, 0, tiled=True)


def shards(
    features, nbr_owner, nbr_row, counts, weight_one, weight_two, w_in, w_rec, gate_bias, cotangent
):
    chips = ("x", "z")
    hbm = pl.BlockSpec(memory_space=pltpu.HBM)
    vmem = pl.BlockSpec(memory_space=pltpu.VMEM)
    x = features[0]
    owner = nbr_owner.reshape(KNB, LANES)
    wanted, rank = call(
        plan_kernel,
        (shaped((CHIPS, RANKS), F32), shaped((KNB, LANES), F32)),
        owner,
        nbr_row.reshape(KNB, LANES),
        in_specs=[hbm] * 2,
        scratch=(
            pltpu.VMEM((KNB, LANES), jnp.int32),
            pltpu.VMEM((KNB, LANES), jnp.int32),
            pltpu.SemaphoreType.DMA((2,)),
        ),
        limit=60,
    )
    asked = exchange(wanted, chips)
    pair = lax.all_gather(x, "core", tiled=True)
    asked, pair = lax.optimization_barrier((asked, pair))
    staged = (pltpu.VMEM((SLOTS, H), BF16), pltpu.SemaphoreType.DMA((BLOCKS,)))
    pick, outgoing = call(
        pick_kernel,
        (shaped((SLOTS, H)), shaped((SLOTS, H))),
        asked,
        pair,
        out_specs=[vmem, hbm],
        scratch=staged,
    )
    snap = lax.axis_index(TM).reshape(1).astype(jnp.int32)
    outgoing, cot, rank, snap = lax.optimization_barrier((outgoing, cotangent, rank, snap))
    arrived = exchange(outgoing.reshape(CHIPS, CAP, H), chips).reshape(SLOTS, H)
    cot = lax.all_gather(cot, "t2", tiled=True)
    comb = call(comb_kernel, shaped((NODE, SLOTS)), rank, owner, counts)
    comb, cot = lax.optimization_barrier((comb, cot))
    x = call(first_kernel, shaped((NODE, H)), comb, arrived, x, counts, weight_one)
    pair = lax.all_gather(x, "core", tiled=True)
    outgoing = call(
        again_kernel, shaped((SLOTS, H)), pick, pair, out_specs=hbm, scratch=staged
    )
    outgoing, cot = lax.optimization_barrier((outgoing, cot))
    arrived = exchange(outgoing.reshape(CHIPS, CAP, H), chips).reshape(SLOTS, H)
    cot = lax.all_gather(cot, "t1", tiled=True)
    cot = lax.all_gather(cot, "t0", tiled=True)
    comb, cot = lax.optimization_barrier((comb, cot))
    copies = call(
        second_kernel, shaped((SNAPS, NODE, H)), comb, arrived, x, counts, weight_two
    )
    xs = exchange(copies, TM[::-1])
    hidden, grads = call(
        chain_kernel,
        (shaped((NODE, H)), shaped((NODE, 4 * H))),
        xs,
        cot,
        w_in,
        w_rec,
        gate_bias.reshape(1, 4 * H),
        snap,
        in_specs=[vmem] * 5 + [pl.BlockSpec(memory_space=pltpu.SMEM)],
        out_specs=[hbm] * 2,
        scratch=(
            pltpu.VMEM((SNAPS, 6, NODE, H), F32),
            pltpu.VMEM((4 * H, H), BF16),
            pltpu.VMEM((SNAPS, NODE, H), BF16),
            pltpu.VMEM((SNAPS, NODE, 4 * H), BF16),
            pltpu.SemaphoreType.DMA((2,)),
        ),
    )
    return hidden[None], grads[None]
def solution(mesh):
    mesh = Mesh(mesh.devices.reshape(2, 2, 2, 8, 4, 2), TM + ("z", "x", "core"))
    acct = ("z", "x", "core")
    return jax.shard_map(
        shards,
        mesh=mesh,
        in_specs=(
            P(TM, acct, None),
            P(TM, acct, None),
            P(TM, acct),
            P(TM, acct),
            P(),
            P(),
            P(),
            P(),
            P(),
            P(TM, acct, None),
        ),
        out_specs=(P(TM, acct, None), P(TM, acct, None)),
        check_vma=False,
    )
```
